32 devices in a mesh: group: 4 (over z), tile: 8 (over y, x, core).
Axes of the slice: x: 2, y: 2, z: 4, core: 2. Of those that a mesh axis runs over, the one named last changes fastest.
Arguments:
- contrast: bfloat16 [4096, 1024], P('tile', 'group'), may hold values from -6 to 6
- incident: bfloat16 [4, 8, 4096, 1024], P('group', None, 'tile'), may hold values from -2.5 to 2.5
- signs: int32 [4, 8, 8], P('group'), may hold values from -1 to 1, as said below
- adjoint: bfloat16 [4, 8, 4096, 1024], P('group', None, 'tile'), may hold values from -1 to 1
- proj: bfloat16 [1024, 256], replicated, may hold values from -0.1875 to 0.1875
- mats: bfloat16 [6, 256, 256], replicated, may hold values from -0.15625 to 0.15625
- offsets: int32 [6], replicated, may hold values from -3 to 3, as said below
- expand: bfloat16 [256, 1024], replicated, may hold values from -0.375 to 0.375
Outputs:
- scattered: bfloat16 [4, 8, 4096, 1024], P('group', None, 'tile')
- gradient: float32 [4096, 1024], P('tile', 'group')
The draws below stay inside these ranges and needn't reach their ends.
Inputs may be any that keep to these rules, and one draw needn't show every extreme that they name: `signs`: each entry is -1 or 1. The offsets are distinct; -3 and 3 both occur.
All inputs are finite; a program needn't handle non-finite values.
Results may differ from the reference program's by a relative error of at most 0.015.
Values may be sent and summed in bfloat16 or wider, within the bound.
No kernel may reach another device: no remote copies, remote signals or barrier semaphores. Data moves between devices by JAX's collectives and lax.ppermute only.
A program may use at most 192 MiB of HBM per device.

```python
import jax
import jax.numpy as jnp
from jax import lax

P_SIZE = 1024
K = 256
E = 8
S = 8
NOFF = 6
BOXES = 4096
GROUPS = 4


def draw_signs(key, part):
    return 2 * jax.random.randint(key, (GROUPS, E, S), 0, 2).astype(jnp.int32) - 1


def draw_offsets(key, part):
    inner = jax.random.permutation(key, jnp.arange(-2, 3, dtype=jnp.int32))
    ends = jnp.array([-3, 3], dtype=jnp.int32)
    return jnp.concatenate([ends, inner[:NOFF - 2]]).astype(jnp.int32)


def with_spikes(result, rng, source, target, parts, factor):
    def block_of(position):
        return (jnp.arange(result.shape[position]) // (result.shape[position] // parts)).reshape((-1,) + (1,) * (result.ndim - 1 - position))

    first = jax.random.permutation(rng, parts)[block_of(target)]
    far = (block_of(target) + parts // 2) % parts
    return jnp.where((block_of(source) == first) | (block_of(source) == far), factor * result, result)


def levels(rng, extent, split, least, largest):
    factor_of = 1.0
    for dim, parts in split:
        heights = jax.random.uniform(jax.random.fold_in(jax.random.fold_in(rng, 6), dim), (parts,), jnp.float32, least / len(split), largest / len(split))
        factor_of = factor_of * jnp.repeat(jnp.exp(heights), extent[dim] // parts).reshape((-1,) + (1,) * (len(extent) - 1 - dim))
    return factor_of


def centred(own_key, dims, deviation, bound, cuts=(), held_as=jnp.bfloat16):
    entries = jax.random.normal(own_key, dims, jnp.float32) * deviation
    if len(cuts) > 0:
        entries = levels(own_key, dims, cuts, -0.22, 0.18) * entries
    return jnp.clip(entries, min=-bound, max=bound).astype(held_as)


def heavy_noise(own_key, extent, width, bound, split, heavy, kind=jnp.bfloat16):
    values = width * jax.random.normal(own_key, extent, jnp.float32)
    if split:
        values = values * levels(own_key, extent, split, -0.22, 0.18)
    return jnp.clip(with_spikes(values, jax.random.fold_in(own_key, 3), *heavy), -bound, bound).astype(kind)


def setup_inputs(seed: int = 0) -> dict:
    streams_of = jax.random.split(jax.random.key(seed), 9)
    contrast = centred(streams_of[0], (BOXES, P_SIZE), 1.0, 6.0, ((0, 8), (1, 4)))
    incident = centred(streams_of[1], (GROUPS, S, BOXES, P_SIZE), 0.35, 2.5, ((0, 4), (2, 8)))
    signs = draw_signs(jax.random.fold_in(streams_of[8], 71), 0)
    adjoint = heavy_noise(streams_of[3], (GROUPS, E, BOXES, P_SIZE), 0.125, 1.0, ((0, 4), (2, 8)), (0, 3, 4, 2.0))
    proj = centred(streams_of[4], (P_SIZE, K), P_SIZE ** -0.5, 0.1875)
    mats = centred(streams_of[5], (NOFF, K, K), (K * NOFF) ** -0.5, 0.15625)
    offsets = draw_offsets(jax.random.fold_in(streams_of[8], 71), 0)
    expand = centred(streams_of[7], (K, P_SIZE), K ** -0.5, 0.375)
    return {"contrast": contrast, "incident": incident, "signs": signs, "adjoint": adjoint, "proj": proj, "mats": mats, "offsets": offsets, "expand": expand}


def reference(contrast, incident, signs, adjoint, proj, mats, offsets, expand):
    nbox = contrast.shape[0]
    cfl = contrast.astype(jnp.float32)

    def one_group(items):
        inc_g, sign_g, adj_g = items
        encoded = jnp.einsum("es,sbp->ebp", sign_g.astype(jnp.float32), inc_g.astype(jnp.float32)).astype(jnp.bfloat16)
        source = (cfl[None] * encoded.astype(jnp.float32)).astype(jnp.bfloat16)
        coeffs = jnp.dot(source.reshape(-1, P_SIZE), proj, preferred_element_type=jnp.float32).reshape(E, nbox, K).astype(jnp.bfloat16)
        padded = jnp.pad(coeffs, ((0, 0), (3, 3), (0, 0)))
        local = jnp.zeros((E, nbox, K), jnp.float32)
        for t in range(NOFF):
            start = (offsets[t] + 3).astype(jnp.int32)
            moved = lax.dynamic_slice_in_dim(padded, start, nbox, 1)
            local = local + jnp.dot(moved.reshape(-1, K), mats[t], preferred_element_type=jnp.float32).reshape(E, nbox, K)
        local = local.astype(jnp.bfloat16)
        field = jnp.dot(local.reshape(-1, K), expand, preferred_element_type=jnp.float32).reshape(E, nbox, P_SIZE)
        total = encoded.astype(jnp.float32) + field
        terms = jnp.sum(adj_g.astype(jnp.float32) * total, axis=0)
        return field.astype(jnp.bfloat16), terms

    scattered, terms = lax.map(one_group, (incident, signs, adjoint))
    return scattered, jnp.sum(terms, axis=0)
```

```python
import functools

import jax
import jax.numpy as jnp
from jax import lax
from jax.experimental import pallas as pl
from jax.experimental.pallas import tpu as pltpu
from jax.sharding import PartitionSpec as P

F32 = jnp.float32
BF16 = jnp.bfloat16
HALO = 3


def low_bit(m):
    return m & -m


def exchange(x, axis, m, count):
    return lax.ppermute(x, axis, [(i, i ^ m) for i in range(count)])


def gather_pieces(x, axis, count):
    pieces = {0: x}
    for m in sorted(range(1, count), key=lambda m: (bin(m).count("1"), -m)):
        b = low_bit(m)
        pieces[m] = exchange(pieces[m ^ b], axis, b, count)
    return [pieces[m] for m in range(count)]


def scatter_pieces(own, parts, axis, count):
    parts = dict(enumerate(parts, start=1))
    received = []
    for m in sorted(range(1, count), key=lambda m: (-bin(m).count("1"), m)):
        b = low_bit(m)
        got = exchange(parts[m], axis, b, count)
        if m == b:
            received.append(got)
        else:
            parts[m ^ b] = (parts[m ^ b].astype(F32) + got.astype(F32)).astype(BF16)
    for got in received:
        own = own + got.astype(F32)
    return own


def same_box(rows, columns, rows_of, columns_of):
    r = lax.broadcasted_iota(jnp.int32, (rows, columns), 0)
    c = lax.broadcasted_iota(jnp.int32, (rows, columns), 1)
    return rows_of(r) == columns_of(c)


def encode_kernel(signs, inc, adj, enc, part, mix):
    count, block, points = inc.shape[1:]
    outs = adj.shape[1]

    @pl.when(pl.program_id(0) == 0)
    def _():
        size = count * block
        r = lax.broadcasted_iota(jnp.int32, (block, size), 0)
        c = lax.broadcasted_iota(jnp.int32, (block, size), 1)
        diagonal = (c % block) == r
        for e in range(outs):
            value = jnp.zeros((block, size), F32)
            for s in range(count):
                value = jnp.where(c // block == s, signs[0, e, s].astype(F32), value)
            mix[e * block:(e + 1) * block, :] = jnp.where(diagonal, value, 0.0).astype(BF16)

    x = inc[0].reshape(count * block, points)
    encoded = jnp.dot(mix[...], x, preferred_element_type=F32).astype(BF16)
    encoded = encoded.reshape(outs, block, points)
    enc[...] = encoded
    part[...] = jnp.sum(adj[0].astype(F32) * encoded.astype(F32), axis=0)


def encode(signs, incident, adjoint, block):
    _, count, nbox, points = incident.shape
    outs = adjoint.shape[1]
    return pl.pallas_call(
        encode_kernel,
        grid=(nbox // block,),
        in_specs=[
            pl.BlockSpec(memory_space=pltpu.SMEM),
            pl.BlockSpec((1, count, block, points), lambda i: (0, 0, i, 0)),
            pl.BlockSpec((1, outs, block, points), lambda i: (0, 0, i, 0)),
        ],
        out_specs=[
            pl.BlockSpec((outs, block, points), lambda i: (0, i, 0)),
            pl.BlockSpec((block, points), lambda i: (i, 0)),
        ],
        out_shape=[
            jax.ShapeDtypeStruct((outs, nbox, points), BF16),
            jax.ShapeDtypeStruct((nbox, points), F32),
        ],
        scratch_shapes=[pltpu.VMEM((outs * block, count * block), BF16)],
        compiler_params=pltpu.CompilerParams(vmem_limit_bytes=32 * 2**20),
        cost_estimate=pl.CostEstimate(
            flops=2 * outs * count * block * nbox * points,
            bytes_accessed=nbox * points * (2 * (2 * outs + count) + 4),
            transcendentals=0,
        ),
        name="encode",
    )(signs, incident, adjoint)


def project_kernel(axis, count, enc, *refs):
    contrasts, (proj, out, order) = refs[:count], refs[count:]
    outs, block, points = enc.shape
    size = outs * block
    share = points // count
    me = lax.axis_index(axis)

    @pl.when(pl.program_id(0) == 0)
    def _():
        r = lax.broadcasted_iota(jnp.int32, (size, size), 0)
        c = lax.broadcasted_iota(jnp.int32, (size, size), 1)
        hit = (r % outs) * block + r // outs == c
        order[...] = jnp.where(hit, 1.0, 0.0).astype(BF16)

    total = None
    for m in range(count):
        start = pl.multiple_of((me ^ m) * share, share)
        source = contrasts[m][...][None] * enc[:, :, pl.ds(start, share)]
        term = jnp.dot(
            source.reshape(size, share), proj[pl.ds(start, share), :], preferred_element_type=F32
        )
        total = term if total is None else total + term
    coeffs = total.astype(BF16)
    out[...] = jnp.dot(order[...], coeffs, preferred_element_type=F32).astype(BF16)


def project(axis, count, enc, pieces, proj, block):
    outs, nbox, points = enc.shape
    width = proj.shape[1]
    share = points // count
    size = outs * block
    return pl.pallas_call(
        functools.partial(project_kernel, axis, count),
        grid=(nbox // block,),
        in_specs=[pl.BlockSpec((outs, block, points), lambda i: (0, i, 0))]
        + [pl.BlockSpec((block, share), lambda i: (i, 0))] * count
        + [pl.BlockSpec((points, width), lambda i: (0, 0))],
        out_specs=pl.BlockSpec((size, width), lambda i: (i, 0)),
        out_shape=jax.ShapeDtypeStruct((outs * nbox, width), BF16),
        scratch_shapes=[pltpu.VMEM((size, size), BF16)],
        compiler_params=pltpu.CompilerParams(vmem_limit_bytes=32 * 2**20),
        cost_estimate=pl.CostEstimate(
            flops=2 * outs * nbox * width * (points + size),
            bytes_accessed=2 * outs * nbox * (points + width),
            transcendentals=0,
        ),
        name="project",
    )(enc, *pieces, proj)


def expand_kernel(axis, count, edge, offsets, coeffs, low, high, mats, expand, adj, part, *refs):
    scattered, own, others = refs[0], refs[1], refs[2:1 + count]
    order, padded, terms = refs[1 + count:]
    _, outs, block, points = adj.shape
    size = outs * block
    share = points // count
    me = lax.axis_index(axis)
    step = pl.program_id(0)
    rows = coeffs.shape[0]

    @pl.when(step == 0)
    def _():
        r = lax.broadcasted_iota(jnp.int32, (size, size), 0)
        c = lax.broadcasted_iota(jnp.int32, (size, size), 1)
        hit = (r % block) * outs + r // block == c
        order[...] = jnp.where(hit, 1.0, 0.0).astype(BF16)
        padded[0:edge, :] = low[...].astype(F32)
        padded[edge:edge + rows, :] = coeffs[...].astype(F32)
        padded[edge + rows:edge + rows + edge, :] = high[...].astype(F32)

    local = None
    for t in range(mats.shape[0]):
        start = pl.multiple_of(step * size + edge + offsets[t] * outs, outs)
        moved = padded[pl.ds(start, size), :].astype(BF16)
        term = jnp.dot(moved, mats[t], preferred_element_type=F32)
        local = term if local is None else local + term
    local = jnp.dot(order[...], local.astype(BF16), preferred_element_type=F32).astype(BF16)
    field = jnp.dot(local, expand[...], preferred_element_type=F32).reshape(outs, block, points)
    scattered[0] = field.astype(BF16)
    terms[...] = part[...] + jnp.sum(adj[0].astype(F32) * field, axis=0)
    for m in range(count):
        start = pl.multiple_of((me ^ m) * share, share)
        piece = terms[:, pl.ds(start, share)]
        if m == 0:
            own[...] = piece
        else:
            others[m - 1][...] = piece.astype(BF16)


def expanded(axis, count, offsets, coeffs, low, high, mats, expand, adjoint, part, block):
    _, outs, nbox, points = adjoint.shape
    width = expand.shape[0]
    share = points // count
    size = outs * block
    edge = low.shape[0]
    return pl.pallas_call(
        functools.partial(expand_kernel, axis, count, edge),
        grid=(nbox // block,),
        in_specs=[
            pl.BlockSpec(memory_space=pltpu.SMEM),
            pl.BlockSpec(coeffs.shape, lambda i: (0, 0)),
            pl.BlockSpec(low.shape, lambda i: (0, 0)),
            pl.BlockSpec(high.shape, lambda i: (0, 0)),
            pl.BlockSpec(mats.shape, lambda i: (0, 0, 0)),
            pl.BlockSpec(expand.shape, lambda i: (0, 0)),
            pl.BlockSpec((1, outs, block, points), lambda i: (0, 0, i, 0)),
            pl.BlockSpec((block, points), lambda i: (i, 0)),
        ],
        out_specs=[
            pl.BlockSpec((1, outs, block, points), lambda i: (0, 0, i, 0)),
        ]
        + [pl.BlockSpec((block, share), lambda i: (i, 0))] * count,
        out_shape=[
            jax.ShapeDtypeStruct((1, outs, nbox, points), BF16),
            jax.ShapeDtypeStruct((nbox, share), F32),
        ]
        + [jax.ShapeDtypeStruct((nbox, share), BF16)] * (count - 1),
        scratch_shapes=[
            pltpu.VMEM((size, size), BF16),
            pltpu.VMEM((coeffs.shape[0] + 2 * edge, width), F32),
            pltpu.VMEM((block, points), F32),
        ],
        compiler_params=pltpu.CompilerParams(vmem_limit_bytes=40 * 2**20),
        cost_estimate=pl.CostEstimate(
            flops=2 * outs * nbox * width * (mats.shape[0] * width + size + points),
            bytes_accessed=nbox * points * (4 * outs + 8),
            transcendentals=0,
        ),
        name="expand",
    )(offsets, coeffs, low, high, mats, expand, adjoint, part)


def on_device(groups, tiles, contrast, incident, signs, adjoint, proj, mats, offsets, expand):
    outs = adjoint.shape[1]
    nbox = contrast.shape[0]
    block = min(256 // outs, nbox)
    edge = 4 * outs
    pieces = gather_pieces(contrast, "group", groups)
    enc, part = encode(signs, incident, adjoint, block)
    coeffs = project("group", groups, enc, pieces, proj, block)
    upward = [(i, i + 1) for i in range(tiles - 1)]
    downward = [(i + 1, i) for i in range(tiles - 1)]
    low = lax.ppermute(coeffs[nbox * outs - edge:], "tile", upward)
    high = lax.ppermute(coeffs[:edge], "tile", downward)
    scattered, own, *parts = expanded(
        "group", groups, offsets, coeffs, low, high, mats, expand, adjoint, part, block
    )
    gradient = scatter_pieces(own, parts, "group", groups)
    return scattered, gradient


def solution(mesh):
    in_specs = (
        P("tile", "group"),
        P("group", None, "tile", None),
        P("group", None, None),
        P("group", None, "tile", None),
        P(),
        P(),
        P(),
        P(),
    )
    out_specs = (P("group", None, "tile", None), P("tile", "group"))
    return jax.shard_map(
        functools.partial(on_device, mesh.shape["group"], mesh.shape["tile"]),
        mesh=mesh,
        in_specs=in_specs,
        out_specs=out_specs,
        check_vma=False,
    )
```

```python
import functools

import jax
import jax.numpy as jnp
from jax import lax
from jax.experimental import pallas as pl
from jax.experimental.pallas import tpu as pltpu
from jax.sharding import PartitionSpec as P

F32 = jnp.float32
BF16 = jnp.bfloat16
ROWS = 16
VMEM = pl.BlockSpec(memory_space=pltpu.VMEM)
SMEM = pl.BlockSpec(memory_space=pltpu.SMEM)
ANY = pl.BlockSpec(memory_space=pl.ANY)


def near(x):
    return pltpu.with_memory_space_constraint(x, pltpu.VMEM)


def in_blocks(segments, size, body):
    done = 0
    for first, extent in segments:
        whole = extent // size
        if whole == 1:
            body(first, done, size)
        elif whole > 1:
            def step(i, carry, first=first, done=done):
                body(
                    pl.multiple_of(first + i * size, ROWS),
                    pl.multiple_of(done + i * size, ROWS),
                    size,
                )
                return carry

            lax.fori_loop(0, whole, step, 0)
        if extent % size:
            body(first + whole * size, done + whole * size, extent % size)
        done += extent


def encode_kernel(block, group, signs, inc, adj, enc, adjv, part, incv, mix, sems):
    count, nbox, points = incv.shape
    outs = enc.shape[0]
    size = count * group
    steps = nbox // block

    def copies(i):
        rows = pl.ds(i * block, block)
        return (
            pltpu.make_async_copy(inc.at[0, :, rows, :], incv.at[:, rows, :], sems.at[0, i]),
            pltpu.make_async_copy(adj.at[0, :, rows, :], adjv.at[:, rows, :], sems.at[1, i]),
        )

    for i in range(steps):
        for copy in copies(i):
            copy.start()

    r = lax.broadcasted_iota(jnp.int32, (group, size), 0)
    c = lax.broadcasted_iota(jnp.int32, (group, size), 1)
    diagonal = (c % group) == r
    for e in range(outs):
        value = jnp.zeros((group, size), F32)
        for s in range(count):
            value = jnp.where(c // group == s, signs[0, e, s].astype(F32), value)
        mix[e * group:(e + 1) * group, :] = jnp.where(diagonal, value, 0.0).astype(BF16)

    def step(i, carry):
        for copy in copies(i):
            copy.wait()
        for j in range(block // group):
            rows = pl.ds(pl.multiple_of(i * block + j * group, ROWS), group)
            x = incv[:, rows, :].reshape(size, points)
            encoded = jnp.dot(mix[...], x, preferred_element_type=F32).astype(BF16)
            encoded = encoded.reshape(outs, group, points)
            enc[:, rows, :] = encoded
            part[rows, :] = jnp.sum(adjv[:, rows, :].astype(F32) * encoded.astype(F32), axis=0)
        return carry

    lax.fori_loop(0, steps, step, 0)


def encode(signs, incident, adjoint, block=64):
    _, count, nbox, points = incident.shape
    outs = adjoint.shape[1]
    group = 256 // count
    return pl.pallas_call(
        functools.partial(encode_kernel, block, group),
        in_specs=[SMEM, ANY, ANY],
        out_specs=[VMEM] * 3,
        out_shape=[
            pltpu.VMEM((outs, nbox, points), BF16),
            pltpu.VMEM((outs, nbox, points), BF16),
            pltpu.VMEM((nbox, points), F32),
        ],
        scratch_shapes=[
            pltpu.VMEM((count, nbox, points), BF16),
            pltpu.VMEM((outs * group, count * group), BF16),
            pltpu.SemaphoreType.DMA((2, nbox // block)),
        ],
        compiler_params=pltpu.CompilerParams(vmem_limit_bytes=32 * 2**20),
        cost_estimate=pl.CostEstimate(
            flops=2 * outs * count * group * nbox * points,
            bytes_accessed=nbox * points * (2 * (2 * outs + count) + 4),
            transcendentals=0,
        ),
        name="encode",
    )(signs, incident, adjoint)


def project_kernel(axis, count, segments, block, enc, *refs):
    contrasts, (proj, out) = refs[:count], refs[count:]
    outs, _, points = enc.shape
    width = proj.shape[1]
    share = points // count
    me = lax.axis_index(axis)
    starts = [pl.multiple_of((me ^ m) * share, share) for m in range(count)]

    def body(first, row, size):
        rows = pl.ds(row, size)
        source = jnp.concatenate(
            [
                contrasts[m][rows, :][None] * enc[:, pl.ds(first, size), pl.ds(starts[m], share)]
                for m in range(count)
            ],
            axis=2,
        ).reshape(outs * size, points)
        weights = jnp.concatenate([proj[pl.ds(starts[m], share), :] for m in range(count)], axis=0)
        coeffs = jnp.dot(source, weights, preferred_element_type=F32)
        out[:, rows, :] = coeffs.astype(BF16).reshape(outs, size, width)

    in_blocks(segments, block, body)


def project(axis, count, segments, enc, pieces, proj, block=128):
    outs, _, points = enc.shape
    width = proj.shape[1]
    nbox = sum(extent for _, extent in segments)
    return pl.pallas_call(
        functools.partial(project_kernel, axis, count, segments, block),
        in_specs=[VMEM] * (count + 2),
        out_specs=VMEM,
        out_shape=pltpu.VMEM((outs, nbox, width), BF16),
        compiler_params=pltpu.CompilerParams(vmem_limit_bytes=16 * 2**20),
        cost_estimate=pl.CostEstimate(
            flops=2 * outs * nbox * width * points,
            bytes_accessed=2 * outs * nbox * width,
            transcendentals=0,
        ),
        name="project",
    )(near(enc), *map(near, pieces), near(proj))


def expand_kernel(axis, count, segments, block, fills, chunk, offsets, *refs):
    sources = refs[:1 + max(f[0] for f in fills)]
    mats, expand, adj, part, _, scattered, own, *others = refs[len(sources):len(sources) + 6 + count]
    padded, ready, terms, sems = refs[len(sources) + 6 + count:]
    outs, _, points = adj.shape
    operators, depth, width = mats.shape
    share = points // count
    me = lax.axis_index(axis)
    halves = padded.shape[0]
    lanes = padded.shape[3]
    edge = ROWS

    for source, begin, extent, place in fills:
        for h in range(halves):
            for e in range(outs):
                padded[h, e, place + edge:place + edge + extent, :] = sources[source][
                    e, begin:begin + extent, h * lanes:(h + 1) * lanes
                ].astype(F32)

    def copy(first, row, size, slot):
        return pltpu.make_async_copy(
            ready.at[:, pl.ds(row, size), :], scattered.at[0, :, pl.ds(first, size), :], sems.at[slot]
        )

    def body(first, row, size):
        moved = [
            padded[h, :, pl.ds(first + edge + offsets[t], size), :]
            .astype(BF16)
            .reshape(outs * size, lanes)
            for t in range(operators)
            for h in range(halves)
        ]
        local = jnp.dot(
            jnp.concatenate(moved, axis=1),
            mats[...].reshape(operators * depth, width),
            preferred_element_type=F32,
        ).astype(BF16)
        rows = pl.ds(row, size)
        for c in range(0, points, chunk):
            columns = slice(c, c + chunk)
            field = jnp.dot(local, expand[:, columns], preferred_element_type=F32)
            field = field.reshape(outs, size, chunk)
            ready[:, rows, columns] = field.astype(BF16)
            terms[0:size, columns] = part[pl.ds(first, size), columns] + jnp.sum(
                adj[:, pl.ds(first, size), columns].astype(F32) * field, axis=0
            )
        for m in range(count):
            start = pl.multiple_of((me ^ m) * share, share)
            piece = terms[0:size, pl.ds(start, share)]
            if m == 0:
                own[rows, :] = piece
            else:
                others[m - 1][rows, :] = piece.astype(BF16)
        copy(first, row, size, lax.div(row, ROWS)).start()

    in_blocks(segments, block, body)
    in_blocks(segments, block, lambda first, row, size: copy(first, row, size, lax.div(row, ROWS)).wait())


def expanded(axis, count, segments, fills, offsets, sources, mats, expand, adj, part, scattered, block=128, chunk=1024):
    outs, nbox, points = adj.shape
    width = expand.shape[0]
    share = points // count
    lanes = min(128, width)
    rows = sum(extent for _, extent in segments)
    alias = {} if scattered is None else {1 + len(sources) + 4: 0}
    if scattered is None:
        scattered = jnp.zeros((8, 128), F32)
    return pl.pallas_call(
        functools.partial(expand_kernel, axis, count, segments, block, fills, chunk),
        in_specs=[SMEM] + [VMEM] * (len(sources) + 4) + [ANY],
        out_specs=[ANY] + [VMEM] * count,
        out_shape=[
            jax.ShapeDtypeStruct((1, outs, nbox, points), BF16),
            pltpu.VMEM((rows, share), F32),
        ]
        + [pltpu.VMEM((rows, share), BF16)] * (count - 1),
        input_output_aliases=alias,
        scratch_shapes=[
            pltpu.VMEM((width // lanes, outs, nbox + 2 * ROWS, lanes), F32),
            pltpu.VMEM((outs, rows, points), BF16),
            pltpu.VMEM((block, points), F32),
            pltpu.SemaphoreType.DMA((rows // ROWS,)),
        ],
        compiler_params=pltpu.CompilerParams(vmem_limit_bytes=30 * 2**20),
        cost_estimate=pl.CostEstimate(
            flops=2 * outs * rows * width * (mats.shape[0] * width + points),
            bytes_accessed=rows * points * 2 * outs,
            transcendentals=0,
        ),
        name="expand",
    )(offsets, *map(near, sources), near(mats), near(expand), near(adj), near(part), scattered)


def exchange(x, axis, m, count):
    return lax.ppermute(x, axis, [(i, i ^ m) for i in range(count)])


def gather_pieces(pieces, axis, count):
    for m in sorted(range(1, count), key=lambda m: (bin(m).count("1"), -m)):
        if m not in pieces:
            pieces[m] = exchange(pieces[m & (m - 1)], axis, m & -m, count)
    return [pieces[m] for m in range(count)]


def scatter_pieces(own, parts, axis, count):
    parts = dict(enumerate(parts, start=1))
    received = []
    for m in sorted(range(1, count), key=lambda m: (-bin(m).count("1"), -m)):
        rest = m & (m - 1)
        got = exchange(parts[m], axis, m & -m, count)
        if rest:
            parts[rest] = (parts[rest].astype(F32) + got.astype(F32)).astype(BF16)
        else:
            received.append(got)
    for got in received:
        own = own + got.astype(F32)
    return own


def on_device(groups, tiles, contrast, incident, signs, adjoint, proj, mats, offsets, expand):
    nbox = contrast.shape[0]
    half = nbox // 2
    projected = [[(0, half), (nbox - ROWS, ROWS)], [(half, half - ROWS)]]
    finished = [[(ROWS, half - 2 * ROWS)], [(0, ROWS), (half - ROWS, half + ROWS)]]
    upward = [(i, i + 1) for i in range(tiles - 1)]
    downward = [(i + 1, i) for i in range(tiles - 1)]

    first = []
    for segments in projected:
        mine = jnp.concatenate([contrast[a:a + n] for a, n in segments], axis=0)
        pieces = {0: mine}
        for m in range(1, groups):
            if m & (m - 1) == 0:
                pieces[m] = exchange(mine, "group", m, groups)
        first.append(pieces)
    enc, adj, part = encode(signs, incident, adjoint)
    enc, first = lax.optimization_barrier((enc, first))

    gathered = gather_pieces(first[0], "group", groups)
    coeffs_a = project("group", groups, projected[0], enc, gathered, proj)
    low = lax.ppermute(coeffs_a[:, half:], "tile", upward)
    high = lax.ppermute(coeffs_a[:, :ROWS], "tile", downward)
    scattered, own_a, *parts_a = expanded(
        "group", groups, finished[0], [(0, 0, half, 0)], offsets, [coeffs_a],
        mats, expand, adj, part, None,
    )
    gathered = gather_pieces(first[1], "group", groups)
    coeffs_b = project("group", groups, projected[1], enc, gathered, proj)
    fills = [(0, 0, 2 * ROWS, 0), (0, half - 2 * ROWS, 2 * ROWS, half - 2 * ROWS)]
    fills += [(0, half, ROWS, nbox - ROWS), (1, 0, half - ROWS, half)]
    fills += [(2, 0, ROWS, -ROWS), (3, 0, ROWS, nbox)]
    grad_a = scatter_pieces(own_a, parts_a, "group", groups)
    scattered, own_b, *parts_b = expanded(
        "group", groups, finished[1], fills, offsets, [coeffs_a, coeffs_b, low, high],
        mats, expand, adj, part, scattered, block=144,
    )
    grad_b = scatter_pieces(own_b, parts_b, "group", groups)
    gradient = jnp.concatenate([grad_b[:ROWS], grad_a, grad_b[ROWS:]], axis=0)
    return scattered, gradient


def solution(mesh):
    in_specs = (
        P("tile", "group"),
        P("group", None, "tile", None),
        P("group", None, None),
        P("group", None, "tile", None),
        P(),
        P(),
        P(),
        P(),
    )
    out_specs = (P("group", None, "tile", None), P("tile", "group"))
    return jax.shard_map(
        functools.partial(on_device, mesh.shape["group"], mesh.shape["tile"]),
        mesh=mesh,
        in_specs=in_specs,
        out_specs=out_specs,
        check_vma=False,
    )
```

```python
import functools

import jax
import jax.numpy as jnp
from jax import lax
from jax.experimental import pallas as pl
from jax.experimental.pallas import tpu as pltpu
from jax.sharding import PartitionSpec as P

F32 = jnp.float32
BF16 = jnp.bfloat16
ROWS = 16
VMEM = pl.BlockSpec(memory_space=pltpu.VMEM)
SMEM = pl.BlockSpec(memory_space=pltpu.SMEM)
ANY = pl.BlockSpec(memory_space=pl.ANY)
HBM = pl.BlockSpec(memory_space=pltpu.HBM)


def near(x):
    return pltpu.with_memory_space_constraint(x, pltpu.VMEM)


def far(x):
    return pltpu.with_memory_space_constraint(x, pltpu.HBM)


def split_kernel(runs, whole, *refs):
    outs, sems = refs[:-1], refs[-1]
    copies = [
        pltpu.make_async_copy(
            whole.at[first:first + extent, :], outs[to].at[row:row + extent, :], sems.at[i]
        )
        for i, (to, row, first, extent) in enumerate(runs)
    ]
    for copy in copies:
        copy.start()
    for copy in copies:
        copy.wait()


def split(x, parts):
    runs, shapes = [], []
    for to, part in enumerate(parts):
        row = 0
        for first, extent in part:
            runs.append((to, row, first, extent))
            row += extent
        shapes.append(pltpu.VMEM((row, x.shape[1]), x.dtype))
    return pl.pallas_call(
        functools.partial(split_kernel, runs),
        in_specs=[HBM],
        out_specs=[VMEM] * len(parts),
        out_shape=shapes,
        scratch_shapes=[pltpu.SemaphoreType.DMA((len(runs),))],
        name="split",
    )(far(x))


def encode_kernel(block, group, signs, inc, enc, incv, mix, sems):
    count, nbox, points = incv.shape
    outs = enc.shape[0]
    size = count * group
    steps = nbox // block

    def copy(i):
        rows = pl.ds(pl.multiple_of(i * block, ROWS), block)
        return pltpu.make_async_copy(inc.at[0, :, rows, :], incv.at[:, rows, :], sems.at[i])

    for i in range(steps):
        copy(i).start()

    r = lax.broadcasted_iota(jnp.int32, (group, size), 0)
    c = lax.broadcasted_iota(jnp.int32, (group, size), 1)
    diagonal = (c % group) == r
    for e in range(outs):
        value = jnp.zeros((group, size), F32)
        for s in range(count):
            value = jnp.where(c // group == s, signs[0, e, s].astype(F32), value)
        mix[e * group:(e + 1) * group, :] = jnp.where(diagonal, value, 0.0).astype(BF16)

    def step(i, carry):
        copy(i).wait()
        for j in range(block // group):
            rows = pl.ds(pl.multiple_of(i * block + j * group, ROWS), group)
            x = incv[:, rows, :].reshape(size, points)
            encoded = jnp.dot(mix[...], x, preferred_element_type=F32).astype(BF16)
            enc[:, rows, :] = encoded.reshape(outs, group, points)
        return carry

    lax.fori_loop(0, steps, step, 0)


def encode(signs, incident, block=64):
    _, count, nbox, points = incident.shape
    outs = signs.shape[1]
    group = 256 // count
    return pl.pallas_call(
        functools.partial(encode_kernel, block, group),
        in_specs=[SMEM, HBM],
        out_specs=VMEM,
        out_shape=pltpu.VMEM((outs, nbox, points), BF16),
        scratch_shapes=[
            pltpu.VMEM((count, nbox, points), BF16),
            pltpu.VMEM((outs * group, count * group), BF16),
            pltpu.SemaphoreType.DMA((nbox // block,)),
        ],
        compiler_params=pltpu.CompilerParams(vmem_limit_bytes=12 * 2**20),
        cost_estimate=pl.CostEstimate(
            flops=2 * outs * count * group * nbox * points,
            bytes_accessed=nbox * points * 2 * count,
            transcendentals=0,
        ),
        name="encode",
    )(signs, far(incident))


def weigh_kernel(block, adj, enc, _, adjv, part, sems):
    nbox = enc.shape[1]
    steps = nbox // block

    def copy(i):
        rows = pl.ds(pl.multiple_of(i * block, ROWS), block)
        return pltpu.make_async_copy(adj.at[0, :, rows, :], adjv.at[:, rows, :], sems.at[i])

    for i in range(steps):
        copy(i).start()

    def step(i, carry):
        copy(i).wait()
        rows = pl.ds(pl.multiple_of(i * block, ROWS), block)
        part[rows, :] = jnp.sum(adjv[:, rows, :].astype(F32) * enc[:, rows, :].astype(F32), axis=0)
        return carry

    lax.fori_loop(0, steps, step, 0)


def weigh(adjoint, enc, after, block=64):
    outs, nbox, points = enc.shape
    return pl.pallas_call(
        functools.partial(weigh_kernel, block),
        in_specs=[HBM, VMEM, VMEM],
        out_specs=[VMEM, VMEM],
        out_shape=[pltpu.VMEM((outs, nbox, points), BF16), pltpu.VMEM((nbox, points), F32)],
        scratch_shapes=[pltpu.SemaphoreType.DMA((nbox // block,))],
        compiler_params=pltpu.CompilerParams(vmem_limit_bytes=8 * 2**20),
        cost_estimate=pl.CostEstimate(
            flops=1, bytes_accessed=1, transcendentals=0
        ),
        name="weigh",
    )(far(adjoint), near(enc), near(after))


def add_kernel(jobs, *refs):
    for out, place, terms in jobs:
        value = None
        for ref, slot, first, extent in terms:
            ref = refs[ref]
            x = ref[first:first + extent, :] if slot is None else ref[slot, first:first + extent, :]
            x = x.astype(F32)
            value = x if value is None else value + x
        refs[out][place:place + value.shape[0], :] = value.astype(refs[out].dtype)


def add(jobs, operands, shapes):
    return pl.pallas_call(
        functools.partial(add_kernel, jobs),
        in_specs=[VMEM] * len(operands),
        out_specs=[VMEM] * len(shapes),
        out_shape=shapes,
        name="add",
    )(*map(near, operands))


def stage_kernel(axis, count, mine, blocks, edges_at, phases, layout, *refs):
    named, at = {}, 0
    for name, number in layout:
        named[name] = refs[at] if number is None else refs[at:at + number]
        at += 1 if number is None else number
    offsets, mats, expand = named["offsets"], named["mats"], named["expand"]
    adj, part = named["adj"], named["part"]
    padded, scattered = named["padded"], named["scattered"]
    ready, held, terms, sems = refs[at:]
    outs, nbox, points = adj.shape
    operators, depth, width = mats.shape
    share = points // count
    halves, _, _, lanes = padded.shape
    me = lax.axis_index(axis)
    starts = [pl.multiple_of((me ^ m) * share, share) for m in range(count)]

    def fill(place, extent, values):
        for h in range(halves):
            padded[h, :, place + ROWS:place + ROWS + extent, :] = values[
                :, :, h * lanes:(h + 1) * lanes
            ].astype(F32)

    if mine:
        enc, proj, contrasts = named["enc"], named["proj"], named["pieces"]
        weights = jnp.concatenate([proj[pl.ds(s, share), :] for s in starts], axis=0)
        for runs in mine:
            source = [
                jnp.concatenate(
                    [
                        contrast[row:row + size, :][None]
                        * enc[:, first:first + size, pl.ds(start, share)]
                        for contrast, start in zip(contrasts, starts)
                    ],
                    axis=2,
                )
                for first, row, size in runs
            ]
            total = sum(size for _, _, size in runs)
            source = jnp.concatenate(source, axis=1).reshape(outs * total, points)
            coeffs = jnp.dot(source, weights, preferred_element_type=F32).astype(BF16)
            coeffs = coeffs.reshape(outs, total, width)
            done = 0
            for first, _, size in runs:
                fill(first, size, coeffs[:, done:done + size, :])
                done += size
    for edge, place in zip(named.get("edges", ()), edges_at):
        for h in range(halves):
            edge[:, :, h * lanes:(h + 1) * lanes] = padded[
                h, :, place + ROWS:place + 2 * ROWS, :
            ].astype(BF16)
    if "low" in named:
        fill(-ROWS, ROWS, named["low"][...])
        fill(nbox, ROWS, named["high"][...])

    def translated(first, size):
        moved = [
            padded[h, :, pl.ds(first + ROWS + offsets[t], size), :]
            .astype(BF16)
            .reshape(outs * size, lanes)
            for t in range(operators)
            for h in range(halves)
        ]
        return jnp.dot(
            jnp.concatenate(moved, axis=1),
            mats[...].reshape(operators * depth, width),
            preferred_element_type=F32,
        ).astype(BF16)

    def copy(i):
        first, size, row = blocks[i]
        return pltpu.make_async_copy(
            ready.at[:, row:row + size, :], scattered.at[0, :, first:first + size, :], sems.at[i]
        )

    def finish(i, local):
        first, size, row = blocks[i]
        field = jnp.dot(local, expand[...], preferred_element_type=F32)
        field = field.reshape(outs, size, points)
        ready[:, row:row + size, :] = field.astype(BF16)
        terms[0:size, :] = part[first:first + size, :] + jnp.sum(
            adj[:, first:first + size, :].astype(F32) * field, axis=0
        )
        named["own"][row:row + size, :] = terms[0:size, pl.ds(starts[0], share)]
        for phase, members in enumerate(phases):
            for slot, m in enumerate(members):
                named["sent"][phase][slot, row:row + size, :] = terms[
                    0:size, pl.ds(starts[m], share)
                ].astype(BF16)

    rows_of = [outs * size for _, size, _ in blocks]
    held[0, 0:rows_of[0], :] = translated(*blocks[0][:2])
    for i in range(len(blocks)):
        if i + 1 < len(blocks):
            following = translated(*blocks[i + 1][:2])
        finish(i, held[i % 2, 0:rows_of[i], :])
        if i + 1 < len(blocks):
            held[(i + 1) % 2, 0:rows_of[i + 1], :] = following
        copy(i).start()
    for i in range(len(blocks)):
        copy(i).wait()


def stage(axis, count, mine, blocks, edges_at, phases, inputs, state, weight=1.0):
    outs, nbox, points = inputs["adj"].shape
    depth, width = inputs["mats"].shape[1:]
    share = points // count
    lanes = min(128, width)
    placed, rows = [], 0
    for first, size in blocks:
        placed.append((first, size, rows))
        rows += size
    most = max(size for _, size in blocks)

    layout, operands, specs = [], [], []
    for name, value in inputs.items():
        many = isinstance(value, (list, tuple))
        layout.append((name, len(value) if many else None))
        for x in value if many else [value]:
            operands.append(x if name == "offsets" else near(x))
            specs.append(SMEM if name == "offsets" else VMEM)
    aliases = {}
    if state is not None:
        layout += [("padded_in", None), ("scattered_in", None)]
        aliases = {len(operands): 0, len(operands) + 1: 1}
        operands += [near(state[0]), state[1]]
        specs += [VMEM, ANY]

    layout += [("padded", None), ("scattered", None), ("own", None), ("sent", len(phases))]
    out_shape = [
        pltpu.VMEM((width // lanes, outs, nbox + 2 * ROWS, lanes), F32),
        jax.ShapeDtypeStruct((1, outs, nbox, points), BF16),
        pltpu.VMEM((rows, share), F32),
    ]
    out_shape += [pltpu.VMEM((len(members), rows, share), BF16) for members in phases]
    out_specs = [VMEM, ANY, VMEM] + [VMEM] * len(phases)
    if edges_at:
        layout.append(("edges", len(edges_at)))
        out_shape += [pltpu.VMEM((outs, ROWS, width), BF16)] * len(edges_at)
        out_specs += [VMEM] * len(edges_at)
    made = sum(size for runs in mine for _, _, size in runs)
    result = pl.pallas_call(
        functools.partial(stage_kernel, axis, count, mine, placed, edges_at, phases, layout),
        in_specs=specs,
        out_specs=out_specs,
        out_shape=out_shape,
        input_output_aliases=aliases,
        scratch_shapes=[
            pltpu.VMEM((outs, rows, points), BF16),
            pltpu.VMEM((2, outs * most, width), BF16),
            pltpu.VMEM((most, points), F32),
            pltpu.SemaphoreType.DMA((len(blocks),)),
        ],
        compiler_params=pltpu.CompilerParams(vmem_limit_bytes=16 * 2**20),
        cost_estimate=pl.CostEstimate(
            flops=int(
                weight * 2 * outs * width
                * (made * points + rows * (inputs["mats"].shape[0] * depth + points))
            ),
            bytes_accessed=int(weight * rows * points * 2 * outs),
            transcendentals=0,
        ),
        name="stage",
    )(*operands)
    state, own, sent = result[:2], result[2], result[3:3 + len(phases)]
    return state, own, sent, result[3 + len(phases):]


def cut_up(first, extent, parts):
    tiles = extent // ROWS
    sizes = [ROWS * (tiles // parts + (i < tiles % parts)) for i in range(parts)]
    return [(first + sum(sizes[:i]), size) for i, size in enumerate(sizes) if size]


def exchange(x, axis, m, count):
    return lax.ppermute(x, axis, [(i, i ^ m) for i in range(count)])


def gather_pieces(pieces, axis, count):
    for m in sorted(range(1, count), key=lambda m: (bin(m).count("1"), -m)):
        if m not in pieces:
            pieces[m] = exchange(pieces[m & (m - 1)], axis, m & -m, count)
    return [pieces[m] for m in range(count)]


def hypercube(count):
    bits = [1 << k for k in range(count.bit_length() - 1)]
    return [[m for m in reversed(range(count)) if m & -m == b] for b in bits]


def folded(members, sent, got, kept):
    for s, m in enumerate(members):
        if m & (m - 1):
            kept[m & (m - 1)] = (kept[m & (m - 1)].astype(F32) + got[s].astype(F32)).astype(BF16)
    return kept


def scatter_steps(sent, axis, count):
    phases = hypercube(count)
    kept = {m: sent[p][s] for p, members in enumerate(phases) for s, m in enumerate(members)}
    final = []
    for p, members in enumerate(phases):
        whole = sent[p] if p == 0 else jnp.stack([kept[m] for m in members])
        got = exchange(whole, axis, 1 << p, count)
        kept = folded(members, sent, got, kept)
        final.append((got, len(members) - 1))
    return final


def first_sums(own, got, sent, after, axis, count):
    phases = hypercube(count)
    came = exchange(sent[0], axis, 1, count)
    rows, share = own.shape
    rows_b = sent[0].shape[1]
    operands = [own] + [x for x, _ in got] + [came] + list(sent[1:]) + [after]
    at = 1 + len(got)
    outs = len(operands)
    jobs = [(outs, 0, [(0, None, 0, rows)] + [(1 + i, slot, 0, rows) for i, (_, slot) in enumerate(got)])]
    shapes = [pltpu.VMEM((rows, share), F32)]
    order = []
    for p, members in enumerate(phases[1:]):
        for s, m in enumerate(members):
            terms = [(at + 1 + p, s, 0, rows_b)]
            if m + 1 in phases[0] and m + 1 < count:
                terms.append((at, phases[0].index(m + 1), 0, rows_b))
            jobs.append((outs + 1 + len(order), 0, terms))
            shapes.append(pltpu.VMEM((rows_b, share), BF16))
            order.append(m)
    total, *kept = add(jobs, operands, shapes)
    return total, (came, dict(zip(order, kept)))


def scatter_last(begun, axis, count):
    came, kept = begun
    phases = hypercube(count)
    final = [(came, len(phases[0]) - 1)]
    for p, members in enumerate(phases):
        if p:
            got = exchange(jnp.stack([kept[m] for m in members]), axis, 1 << p, count)
            kept = folded(members, None, got, kept)
            final.append((got, len(members) - 1))
    return final


def scatter_direct(sent, axis, count):
    return [(exchange(x, axis, m, count), 0) for m, x in enumerate(sent, start=1)]


def on_device(groups, tiles, contrast, incident, signs, adjoint, proj, mats, offsets, expand):
    nbox = contrast.shape[0]
    half = nbox // 2
    cut, last = half + ROWS, nbox - ROWS
    third = half + (last - half) // ROWS // 2 * ROWS
    upward = [(i, i + 1) for i in range(tiles - 1)]
    downward = [(i + 1, i) for i in range(tiles - 1)]

    def started(x):
        return {0: x} | {
            m: exchange(x, "group", m, groups) for m in reversed(range(1, groups)) if not m & (m - 1)
        }

    contrast_a, contrast_b = split(contrast, [[(0, cut), (last, ROWS)], [(cut, last - cut)]])
    pieces_a = started(contrast_a)
    enc = encode(signs, incident)
    top, enc, contrast_b = lax.optimization_barrier((pieces_a[groups // 2], enc, contrast_b))
    pieces_a[groups // 2] = top
    adj, part = weigh(adjoint, enc, top)
    pieces_a = gather_pieces(pieces_a, "group", groups)
    pieces_b = [contrast_b] + [exchange(contrast_b, "group", m, groups) for m in range(1, groups)]

    common = dict(offsets=offsets, mats=mats, expand=expand, adj=adj, part=part)
    mine = [[(first, first, size)] for first, size in cut_up(0, cut, 2)]
    mine[-1].append((last, cut, ROWS))
    state, own_a, sent_a, edges = stage(
        "group", groups, mine, cut_up(ROWS, half - ROWS, 3), (0, last),
        hypercube(groups), common | dict(enc=enc, proj=proj, pieces=pieces_a), None, weight=0.0,
    )
    high = lax.ppermute(edges[0], "tile", downward)
    low = lax.ppermute(edges[1], "tile", upward)

    mine = [[(first, first - cut, size)] for first, size in cut_up(cut, last - cut, 2)]
    state, own_b, sent_b, _ = stage(
        "group", groups, mine, cut_up(half, third - half, 2), (),
        hypercube(groups), common | dict(enc=enc, proj=proj, pieces=pieces_b), state, weight=1.0,
    )
    got_a = scatter_steps(sent_a, "group", groups)
    state, own_c, sent_c, _ = stage(
        "group", groups, [], cut_up(third, nbox - third, 2) + [(0, ROWS)], (),
        [[m] for m in range(1, groups)], common | dict(low=low, high=high), state, weight=1.0,
    )
    share = own_a.shape[1]
    rows_a, rows_b, rows_c = half - ROWS, third - half, nbox - third
    done_a, sent_b = first_sums(own_a, got_a, sent_b, sent_c[0], "group", groups)
    got_b = scatter_last(sent_b, "group", groups)
    got_c = scatter_direct(sent_c, "group", groups)

    operands = [done_a, own_b] + [x for x, _ in got_b] + [own_c] + [x for x, _ in got_c]
    at_c = 2 + len(got_b)
    out = len(operands)
    pick_b = [(1, None)] + [(2 + i, slot) for i, (_, slot) in enumerate(got_b)]
    pick_c = [(at_c, None)] + [(at_c + 1 + i, slot) for i, (_, slot) in enumerate(got_c)]
    jobs = [
        (out, 0, [(ref, slot, rows_c, ROWS) for ref, slot in pick_c]),
        (out, ROWS, [(0, None, 0, rows_a)]),
        (out, half, [(ref, slot, 0, rows_b) for ref, slot in pick_b]),
        (out, third, [(ref, slot, 0, rows_c) for ref, slot in pick_c]),
    ]
    (gradient,) = add(jobs, operands, [jax.ShapeDtypeStruct((nbox, share), F32)])
    return state[1], gradient


def solution(mesh):
    in_specs = (
        P("tile", "group"),
        P("group", None, "tile", None),
        P("group", None, None),
        P("group", None, "tile", None),
        P(),
        P(),
        P(),
        P(),
    )
    out_specs = (P("group", None, "tile", None), P("tile", "group"))
    return jax.shard_map(
        functools.partial(on_device, mesh.shape["group"], mesh.shape["tile"]),
        mesh=mesh,
        in_specs=in_specs,
        out_specs=out_specs,
        check_vma=False,
    )
```

```python
import functools

import jax
import jax.numpy as jnp
from jax import lax
from jax.experimental import pallas as pl
from jax.experimental.pallas import tpu as pltpu
from jax.sharding import PartitionSpec as P

F32 = jnp.float32
BF16 = jnp.bfloat16
ROWS = 16
VMEM = pl.BlockSpec(memory_space=pltpu.VMEM)
SMEM = pl.BlockSpec(memory_space=pltpu.SMEM)
ANY = pl.BlockSpec(memory_space=pl.ANY)
HBM = pl.BlockSpec(memory_space=pltpu.HBM)


def near(x):
    return pltpu.with_memory_space_constraint(x, pltpu.VMEM)


def far(x):
    return pltpu.with_memory_space_constraint(x, pltpu.HBM)


def split_kernel(runs, whole, *refs):
    outs, sems = refs[:-1], refs[-1]
    copies = [
        pltpu.make_async_copy(
            whole.at[first:first + extent, :], outs[to].at[row:row + extent, :], sems.at[i]
        )
        for i, (to, row, first, extent) in enumerate(runs)
    ]
    for copy in copies:
        copy.start()
    for copy in copies:
        copy.wait()


def split(x, parts):
    runs, shapes = [], []
    for to, part in enumerate(parts):
        row = 0
        for first, extent in part:
            runs.append((to, row, first, extent))
            row += extent
        shapes.append(pltpu.VMEM((row, x.shape[1]), x.dtype))
    return pl.pallas_call(
        functools.partial(split_kernel, runs),
        in_specs=[HBM],
        out_specs=[VMEM] * len(parts),
        out_shape=shapes,
        scratch_shapes=[pltpu.SemaphoreType.DMA((len(runs),))],
        compiler_params=pltpu.CompilerParams(vmem_limit_bytes=4 * 2**20),
        name="split",
    )(far(x))


def encode_kernel(block, group, weighed, signs_in, inc, adj, enc, adjv, part, signs, incv, mix, sems):
    count, nbox, points = incv.shape
    outs = enc.shape[0]
    size = count * group
    steps = nbox // block

    def copies(i):
        rows = pl.ds(pl.multiple_of(i * block, ROWS), block)
        inc_copy = pltpu.make_async_copy(inc.at[0, :, rows, :], incv.at[:, rows, :], sems.at[0, i])
        adj_copy = pltpu.make_async_copy(adj.at[0, :, rows, :], adjv.at[:, rows, :], sems.at[1, i])
        return inc_copy, adj_copy

    signs_copy = pltpu.make_async_copy(signs_in, signs, sems.at[0, steps])
    signs_copy.start()
    for i in range(steps):
        inc_copy, adj_copy = copies(i)
        inc_copy.start()
        if i < weighed:
            adj_copy.start()
    signs_copy.wait()

    r = lax.broadcasted_iota(jnp.int32, (group, size), 0)
    c = lax.broadcasted_iota(jnp.int32, (group, size), 1)
    diagonal = (c % group) == r
    for e in range(outs):
        value = jnp.zeros((group, size), F32)
        for s in range(count):
            value = jnp.where(c // group == s, signs[0, e, s].astype(F32), value)
        mix[e * group:(e + 1) * group, :] = jnp.where(diagonal, value, 0.0).astype(BF16)

    def step(i, carry, weigh):
        inc_copy, adj_copy = copies(i)
        inc_copy.wait()
        if weigh:
            adj_copy.wait()
        for j in range(block // group):
            rows = pl.ds(pl.multiple_of(i * block + j * group, ROWS), group)
            x = incv[:, rows, :].reshape(size, points)
            encoded = jnp.dot(mix[...], x, preferred_element_type=F32).astype(BF16)
            encoded = encoded.reshape(outs, group, points)
            enc[:, rows, :] = encoded
            if weigh:
                part[rows, :] = jnp.sum(adjv[:, rows, :].astype(F32) * encoded.astype(F32), axis=0)
        return carry

    lax.fori_loop(0, weighed, functools.partial(step, weigh=True), 0)
    lax.fori_loop(weighed, steps, functools.partial(step, weigh=False), 0)


def encode(signs, incident, adjoint, weighed, block=64):
    _, count, nbox, points = incident.shape
    outs = adjoint.shape[1]
    group = 256 // count
    return pl.pallas_call(
        functools.partial(encode_kernel, block, group, weighed // block),
        in_specs=[HBM, HBM, HBM],
        out_specs=[VMEM] * 3,
        out_shape=[
            pltpu.VMEM((outs, nbox, points), BF16),
            pltpu.VMEM((outs, nbox, points), BF16),
            pltpu.VMEM((nbox, points), F32),
        ],
        scratch_shapes=[
            pltpu.SMEM(signs.shape, signs.dtype),
            pltpu.VMEM((count, nbox, points), BF16),
            pltpu.VMEM((outs * group, count * group), BF16),
            pltpu.SemaphoreType.DMA((2, nbox // block + 1)),
        ],
        compiler_params=pltpu.CompilerParams(vmem_limit_bytes=12 * 2**20),
        cost_estimate=pl.CostEstimate(
            flops=2 * outs * count * group * nbox * points,
            bytes_accessed=nbox * points * 2 * count,
            transcendentals=0,
        ),
        name="encode",
    )(far(signs), far(incident), far(adjoint))


def weigh_kernel(block, first, adj, enc, _, adj_in, part_in, adjv, part, sems):
    nbox = enc.shape[1]
    steps = nbox // block

    def copy(i):
        rows = pl.ds(pl.multiple_of(i * block, ROWS), block)
        return pltpu.make_async_copy(adj.at[0, :, rows, :], adjv.at[:, rows, :], sems.at[i])

    for i in range(first, steps):
        copy(i).start()

    def step(i, carry):
        copy(i).wait()
        rows = pl.ds(pl.multiple_of(i * block, ROWS), block)
        part[rows, :] = jnp.sum(adjv[:, rows, :].astype(F32) * enc[:, rows, :].astype(F32), axis=0)
        return carry

    lax.fori_loop(first, steps, step, 0)


def weigh(adjoint, enc, adj, part, weighed, after, block=32):
    outs, nbox, points = enc.shape
    return pl.pallas_call(
        functools.partial(weigh_kernel, block, weighed // block),
        in_specs=[HBM] + [VMEM] * 4,
        out_specs=[VMEM, VMEM],
        out_shape=[pltpu.VMEM((outs, nbox, points), BF16), pltpu.VMEM((nbox, points), F32)],
        input_output_aliases={3: 0, 4: 1},
        scratch_shapes=[pltpu.SemaphoreType.DMA((nbox // block,))],
        compiler_params=pltpu.CompilerParams(vmem_limit_bytes=8 * 2**20),
        cost_estimate=pl.CostEstimate(flops=1, bytes_accessed=1, transcendentals=0),
        name="weigh",
    )(far(adjoint), near(enc), near(after), near(adj), near(part))


def add_kernel(jobs, *refs):
    for out, place, terms in jobs:
        value = None
        for ref, slot, first, extent in terms:
            ref = refs[ref]
            x = ref[first:first + extent, :] if slot is None else ref[slot, first:first + extent, :]
            x = x.astype(F32)
            value = x if value is None else value + x
        refs[out][place:place + value.shape[0], :] = value.astype(refs[out].dtype)


def add(jobs, operands, shapes):
    return pl.pallas_call(
        functools.partial(add_kernel, jobs),
        in_specs=[VMEM] * len(operands),
        out_specs=[VMEM] * len(shapes),
        out_shape=shapes,
        compiler_params=pltpu.CompilerParams(vmem_limit_bytes=4 * 2**20),
        name="add",
    )(*map(near, operands))


def leaving(ready, scattered, segments, sems):
    copies, row = [], 0
    for i, (first, size) in enumerate(segments):
        copies.append(
            pltpu.make_async_copy(
                ready.at[:, row:row + size, :], scattered.at[0, :, first:first + size, :], sems.at[i]
            )
        )
        row += size
    return copies


def stage_kernel(axis, count, mine, blocks, edges_at, phases, layout, *refs):
    named, at = {}, 0
    for name, number in layout:
        named[name] = refs[at] if number is None else refs[at:at + number]
        at += 1 if number is None else number
    offsets, mats, expand = named["offsets"], named["mats"], named["expand"]
    adj, part = named["adj"], named["part"]
    padded, ready = named["padded"], named["ready"]
    held, terms = refs[at:]
    outs, nbox, points = adj.shape
    operators, depth, width = mats.shape
    share = points // count
    halves, _, _, lanes = padded.shape
    me = lax.axis_index(axis)
    starts = [pl.multiple_of((me ^ m) * share, share) for m in range(count)]

    def fill(place, extent, values):
        for h in range(halves):
            padded[h, :, place + ROWS:place + ROWS + extent, :] = values[
                :, :, h * lanes:(h + 1) * lanes
            ].astype(F32)

    if mine:
        enc, proj, contrasts = named["enc"], named["proj"], named["pieces"]
        weights = jnp.concatenate([proj[pl.ds(s, share), :] for s in starts], axis=0)
        for runs in mine:
            source = [
                jnp.concatenate(
                    [
                        contrast[row:row + size, :][None]
                        * enc[:, first:first + size, pl.ds(start, share)]
                        for contrast, start in zip(contrasts, starts)
                    ],
                    axis=2,
                )
                for first, row, size in runs
            ]
            total = sum(size for _, _, size in runs)
            source = jnp.concatenate(source, axis=1).reshape(outs * total, points)
            coeffs = jnp.dot(source, weights, preferred_element_type=F32).astype(BF16)
            coeffs = coeffs.reshape(outs, total, width)
            done = 0
            for first, _, size in runs:
                fill(first, size, coeffs[:, done:done + size, :])
                done += size
    for edge, place in zip(named.get("edges", ()), edges_at):
        for h in range(halves):
            edge[:, :, h * lanes:(h + 1) * lanes] = padded[
                h, :, place + ROWS:place + 2 * ROWS, :
            ].astype(BF16)
    if "low" in named:
        fill(-ROWS, ROWS, named["low"][...])
        fill(nbox, ROWS, named["high"][...])

    def translated(first, size):
        moved = [
            padded[h, :, pl.ds(first + ROWS + offsets[t], size), :]
            .astype(BF16)
            .reshape(outs * size, lanes)
            for t in range(operators)
            for h in range(halves)
        ]
        return jnp.dot(
            jnp.concatenate(moved, axis=1),
            mats[...].reshape(operators * depth, width),
            preferred_element_type=F32,
        ).astype(BF16)

    def finish(i, local):
        first, size, row = blocks[i]
        field = jnp.dot(local, expand[...], preferred_element_type=F32)
        field = field.reshape(outs, size, points)
        ready[:, row:row + size, :] = field.astype(BF16)
        terms[0:size, :] = part[first:first + size, :] + jnp.sum(
            adj[:, first:first + size, :].astype(F32) * field, axis=0
        )
        named["own"][row:row + size, :] = terms[0:size, pl.ds(starts[0], share)]
        for phase, members in enumerate(phases):
            for slot, m in enumerate(members):
                named["sent"][phase][slot, row:row + size, :] = terms[
                    0:size, pl.ds(starts[m], share)
                ].astype(BF16)

    rows_of = [outs * size for _, size, _ in blocks]
    held[0, 0:rows_of[0], :] = translated(*blocks[0][:2])
    for i in range(len(blocks)):
        if i + 1 < len(blocks):
            following = translated(*blocks[i + 1][:2])
        finish(i, held[i % 2, 0:rows_of[i], :])
        if i + 1 < len(blocks):
            held[(i + 1) % 2, 0:rows_of[i + 1], :] = following


def stage(axis, count, mine, blocks, edges_at, phases, inputs, state, weight=1.0):
    outs, nbox, points = inputs["adj"].shape
    depth, width = inputs["mats"].shape[1:]
    share = points // count
    lanes = min(128, width)
    placed, rows = [], 0
    for first, size in blocks:
        placed.append((first, size, rows))
        rows += size
    most = max(size for _, size in blocks)

    layout, operands, specs = [], [], []
    for name, value in inputs.items():
        many = isinstance(value, (list, tuple))
        layout.append((name, len(value) if many else None))
        for x in value if many else [value]:
            operands.append(x if name == "offsets" else near(x))
            specs.append(SMEM if name == "offsets" else VMEM)
    aliases = {}
    if state is not None:
        layout.append(("padded_in", None))
        aliases = {len(operands): 0}
        operands.append(near(state))
        specs.append(VMEM)

    layout += [("padded", None), ("ready", None), ("own", None), ("sent", len(phases))]
    out_shape = [
        pltpu.VMEM((width // lanes, outs, nbox + 2 * ROWS, lanes), F32),
        pltpu.VMEM((outs, rows, points), BF16),
        pltpu.VMEM((rows, share), F32),
    ]
    out_shape += [pltpu.VMEM((len(members), rows, share), BF16) for members in phases]
    out_specs = [VMEM] * 3 + [VMEM] * len(phases)
    if edges_at:
        layout.append(("edges", len(edges_at)))
        out_shape += [pltpu.VMEM((outs, ROWS, width), BF16)] * len(edges_at)
        out_specs += [VMEM] * len(edges_at)
    made = sum(size for runs in mine for _, _, size in runs)
    result = pl.pallas_call(
        functools.partial(stage_kernel, axis, count, mine, placed, edges_at, phases, layout),
        in_specs=specs,
        out_specs=out_specs,
        out_shape=out_shape,
        input_output_aliases=aliases,
        scratch_shapes=[
            pltpu.VMEM((2, outs * most, width), BF16),
            pltpu.VMEM((most, points), F32),
        ],
        compiler_params=pltpu.CompilerParams(vmem_limit_bytes=16 * 2**20),
        cost_estimate=pl.CostEstimate(
            flops=int(
                weight * 2 * outs * width
                * (made * points + rows * (inputs["mats"].shape[0] * depth + points))
            ),
            bytes_accessed=int(weight * rows * points * 2 * outs),
            transcendentals=0,
        ),
        name="stage",
    )(*operands)
    padded, ready, own = result[:3]
    return padded, (ready, joined(blocks)), own, result[3:3 + len(phases)], result[3 + len(phases):]


def joined(blocks):
    segments = []
    for first, size in blocks:
        if segments and sum(segments[-1]) == first:
            segments[-1] = (segments[-1][0], segments[-1][1] + size)
        else:
            segments.append((first, size))
    return segments


def flush_kernel(segments, *refs):
    scattered, sems = refs[-2:]
    copies = []
    for ready, held in zip(refs, segments):
        copies += leaving(ready, scattered, held, sems.at[pl.ds(len(copies), len(held))])
    for copy in copies:
        copy.start()
    for copy in copies:
        copy.wait()


def flush(fields, nbox, after):
    outs, _, points = fields[0][0].shape
    segments = [held for _, held in fields]
    return pl.pallas_call(
        functools.partial(flush_kernel, segments),
        in_specs=[VMEM] * (len(fields) + 1),
        out_specs=HBM,
        out_shape=jax.ShapeDtypeStruct((1, outs, nbox, points), BF16),
        scratch_shapes=[pltpu.SemaphoreType.DMA((sum(map(len, segments)),))],
        compiler_params=pltpu.CompilerParams(vmem_limit_bytes=4 * 2**20),
        cost_estimate=pl.CostEstimate(flops=1, bytes_accessed=1, transcendentals=0),
        name="flush",
    )(*[near(ready) for ready, _ in fields], near(after))


def cut_up(first, extent, parts):
    tiles = extent // ROWS
    sizes = [ROWS * (tiles // parts + (i < tiles % parts)) for i in range(parts)]
    return [(first + sum(sizes[:i]), size) for i, size in enumerate(sizes) if size]


def exchange(x, axis, m, count):
    return lax.ppermute(x, axis, [(i, i ^ m) for i in range(count)])


def gather_pieces(pieces, axis, count):
    for m in sorted(range(1, count), key=lambda m: (bin(m).count("1"), -m)):
        if m not in pieces:
            pieces[m] = exchange(pieces[m & (m - 1)], axis, m & -m, count)
    return [pieces[m] for m in range(count)]


def hypercube(count):
    bits = [1 << k for k in range(count.bit_length() - 1)]
    return [[m for m in reversed(range(count)) if m & -m == b] for b in bits]


def folded(members, sent, got, kept):
    for s, m in enumerate(members):
        if m & (m - 1):
            kept[m & (m - 1)] = (kept[m & (m - 1)].astype(F32) + got[s].astype(F32)).astype(BF16)
    return kept


def scatter_steps(sent, axis, count):
    phases = hypercube(count)
    kept = {m: sent[p][s] for p, members in enumerate(phases) for s, m in enumerate(members)}
    final = []
    for p, members in enumerate(phases):
        whole = sent[p] if p == 0 else jnp.stack([kept[m] for m in members])
        got = exchange(whole, axis, 1 << p, count)
        kept = folded(members, sent, got, kept)
        final.append((got, len(members) - 1))
    return final


def first_sums(own, got, sent, after, axis, count):
    phases = hypercube(count)
    came = exchange(sent[0], axis, 1, count)
    rows, share = own.shape
    rows_b = sent[0].shape[1]
    operands = [own] + [x for x, _ in got] + [came] + list(sent[1:]) + [after]
    at = 1 + len(got)
    outs = len(operands)
    jobs = [(outs, 0, [(0, None, 0, rows)] + [(1 + i, slot, 0, rows) for i, (_, slot) in enumerate(got)])]
    shapes = [pltpu.VMEM((rows, share), F32)]
    order = []
    for p, members in enumerate(phases[1:]):
        for s, m in enumerate(members):
            terms = [(at + 1 + p, s, 0, rows_b)]
            if m + 1 in phases[0] and m + 1 < count:
                terms.append((at, phases[0].index(m + 1), 0, rows_b))
            jobs.append((outs + 1 + len(order), 0, terms))
            shapes.append(pltpu.VMEM((rows_b, share), BF16))
            order.append(m)
    total, *kept = add(jobs, operands, shapes)
    return total, (came, dict(zip(order, kept)))


def scatter_last(begun, axis, count):
    came, kept = begun
    phases = hypercube(count)
    final = [(came, len(phases[0]) - 1)]
    for p, members in enumerate(phases):
        if p:
            got = exchange(jnp.stack([kept[m] for m in members]), axis, 1 << p, count)
            kept = folded(members, None, got, kept)
            final.append((got, len(members) - 1))
    return final


def scatter_direct(sent, axis, count):
    return [(exchange(x, axis, m, count), 0) for m, x in enumerate(sent, start=1)]


def on_device(groups, tiles, contrast, incident, signs, adjoint, proj, mats, offsets, expand):
    nbox = contrast.shape[0]
    half = nbox // 32 * 15
    cut, last = half + ROWS, nbox - ROWS
    third = nbox // 32 * 23
    upward = [(i, i + 1) for i in range(tiles - 1)]
    downward = [(i + 1, i) for i in range(tiles - 1)]

    contrast_a, contrast_b = split(contrast, [[(0, cut), (last, ROWS)], [(cut, last - cut)]])
    far_side = groups // 2
    first = exchange(contrast_a, "group", 1, groups)
    top = exchange(contrast_a, "group", far_side, groups)
    weighed = nbox // 2
    enc, adj, part = encode(signs, incident, adjoint, weighed)
    top, first, enc = lax.optimization_barrier((top, first, enc))
    pieces_a = gather_pieces({0: contrast_a, 1: first, far_side: top}, "group", groups)
    adj, part = weigh(adjoint, enc, adj, part, weighed, top)
    part, contrast_b = lax.optimization_barrier((part, contrast_b))
    pieces_b = [contrast_b] + [exchange(contrast_b, "group", m, groups) for m in range(1, groups)]

    common = dict(offsets=offsets, mats=mats, expand=expand, adj=adj, part=part)
    mine = [[(first, first, size)] for first, size in cut_up(0, cut, 2)]
    mine[-1].append((last, cut, ROWS))
    state, field_a, own_a, sent_a, edges = stage(
        "group", groups, mine, cut_up(ROWS, half - ROWS, 3), (0, last),
        hypercube(groups), common | dict(enc=enc, proj=proj, pieces=pieces_a), None, weight=0.0,
    )
    high = lax.ppermute(edges[0], "tile", downward)
    low = lax.ppermute(edges[1], "tile", upward)

    mine = [[(first, first - cut, size)] for first, size in cut_up(cut, last - cut, 2)]
    state, field_b, own_b, sent_b, _ = stage(
        "group", groups, mine, cut_up(half, third - half, 2), (),
        hypercube(groups), common | dict(enc=enc, proj=proj, pieces=pieces_b), state, weight=1.0,
    )
    got_a = scatter_steps(sent_a, "group", groups)
    _, field_c, own_c, sent_c, _ = stage(
        "group", groups, [], cut_up(third, nbox - third, 2) + [(0, ROWS)], (),
        [[m] for m in range(1, groups)], common | dict(low=low, high=high), state, weight=1.0,
    )
    share = own_a.shape[1]
    rows_a, rows_b, rows_c = half - ROWS, third - half, nbox - third
    done_a, sent_b = first_sums(own_a, got_a, sent_b, sent_c[0], "group", groups)
    got_b = scatter_last(sent_b, "group", groups)
    got_c = scatter_direct(sent_c, "group", groups)

    operands = [done_a, own_b] + [x for x, _ in got_b] + [own_c] + [x for x, _ in got_c]
    at_c = 2 + len(got_b)
    out = len(operands)
    pick_b = [(1, None)] + [(2 + i, slot) for i, (_, slot) in enumerate(got_b)]
    pick_c = [(at_c, None)] + [(at_c + 1 + i, slot) for i, (_, slot) in enumerate(got_c)]
    jobs = [
        (out, 0, [(ref, slot, rows_c, ROWS) for ref, slot in pick_c]),
        (out, ROWS, [(0, None, 0, rows_a)]),
        (out, half, [(ref, slot, 0, rows_b) for ref, slot in pick_b]),
        (out, third, [(ref, slot, 0, rows_c) for ref, slot in pick_c]),
    ]
    (gradient,) = add(jobs, operands, [jax.ShapeDtypeStruct((nbox, share), F32)])
    scattered = flush([field_a, field_b, field_c], nbox, got_c[0][0])
    return scattered, gradient


def solution(mesh):
    in_specs = (
        P("tile", "group"),
        P("group", None, "tile", None),
        P("group", None, None),
        P("group", None, "tile", None),
        P(),
        P(),
        P(),
        P(),
    )
    out_specs = (P("group", None, "tile", None), P("tile", "group"))
    return jax.shard_map(
        functools.partial(on_device, mesh.shape["group"], mesh.shape["tile"]),
        mesh=mesh,
        in_specs=in_specs,
        out_specs=out_specs,
        check_vma=False,
    )
```

```python
import functools

import jax
import jax.numpy as jnp
from jax import lax
from jax.experimental import pallas as pl
from jax.experimental.pallas import tpu as pltpu
from jax.sharding import PartitionSpec as P

F32 = jnp.float32
BF16 = jnp.bfloat16
ROWS = 16
VMEM = pl.BlockSpec(memory_space=pltpu.VMEM)
SMEM = pl.BlockSpec(memory_space=pltpu.SMEM)
ANY = pl.BlockSpec(memory_space=pl.ANY)
HBM = pl.BlockSpec(memory_space=pltpu.HBM)


def near(x):
    return pltpu.with_memory_space_constraint(x, pltpu.VMEM)


def far(x):
    return pltpu.with_memory_space_constraint(x, pltpu.HBM)


def split_kernel(runs, whole, *refs):
    outs, sems = refs[:-1], refs[-1]
    copies = [
        pltpu.make_async_copy(
            whole.at[first:first + extent, :], outs[to].at[row:row + extent, :], sems.at[i]
        )
        for i, (to, row, first, extent) in enumerate(runs)
    ]
    for copy in copies:
        copy.start()
    for copy in copies:
        copy.wait()


def split(x, parts):
    runs, shapes = [], []
    for to, part in enumerate(parts):
        row = 0
        for first, extent in part:
            runs.append((to, row, first, extent))
            row += extent
        shapes.append(pltpu.VMEM((row, x.shape[1]), x.dtype))
    return pl.pallas_call(
        functools.partial(split_kernel, runs),
        in_specs=[HBM],
        out_specs=[VMEM] * len(parts),
        out_shape=shapes,
        scratch_shapes=[pltpu.SemaphoreType.DMA((len(runs),))],
        compiler_params=pltpu.CompilerParams(vmem_limit_bytes=4 * 2**20),
        name="split",
    )(far(x))


def encode_kernel(block, group, weighed, signs_in, inc, adj, enc, adjv, part, signs, incv, mix, sems):
    count, nbox, points = incv.shape
    outs = enc.shape[0]
    size = count * group
    steps = nbox // block

    def copies(i):
        rows = pl.ds(pl.multiple_of(i * block, ROWS), block)
        inc_copy = pltpu.make_async_copy(inc.at[0, :, rows, :], incv.at[:, rows, :], sems.at[0, i])
        adj_copy = pltpu.make_async_copy(adj.at[0, :, rows, :], adjv.at[:, rows, :], sems.at[1, i])
        return inc_copy, adj_copy

    signs_copy = pltpu.make_async_copy(signs_in, signs, sems.at[0, steps])
    signs_copy.start()
    for i in range(steps):
        inc_copy, adj_copy = copies(i)
        inc_copy.start()
        if i < weighed:
            adj_copy.start()
    signs_copy.wait()

    r = lax.broadcasted_iota(jnp.int32, (group, size), 0)
    c = lax.broadcasted_iota(jnp.int32, (group, size), 1)
    diagonal = (c % group) == r
    for e in range(outs):
        value = jnp.zeros((group, size), F32)
        for s in range(count):
            value = jnp.where(c // group == s, signs[0, e, s].astype(F32), value)
        mix[e * group:(e + 1) * group, :] = jnp.where(diagonal, value, 0.0).astype(BF16)

    def step(i, carry, weigh):
        inc_copy, adj_copy = copies(i)
        inc_copy.wait()
        if weigh:
            adj_copy.wait()
        for j in range(block // group):
            rows = pl.ds(pl.multiple_of(i * block + j * group, ROWS), group)
            x = incv[:, rows, :].reshape(size, points)
            encoded = jnp.dot(mix[...], x, preferred_element_type=F32).astype(BF16)
            encoded = encoded.reshape(outs, group, points)
            enc[:, rows, :] = encoded
            if weigh:
                part[rows, :] = jnp.sum(adjv[:, rows, :].astype(F32) * encoded.astype(F32), axis=0)
        return carry

    lax.fori_loop(0, weighed, functools.partial(step, weigh=True), 0)
    lax.fori_loop(weighed, steps, functools.partial(step, weigh=False), 0)


def encode(signs, incident, adjoint, weighed, block=64):
    _, count, nbox, points = incident.shape
    outs = adjoint.shape[1]
    group = 256 // count
    return pl.pallas_call(
        functools.partial(encode_kernel, block, group, weighed // block),
        in_specs=[HBM, HBM, HBM],
        out_specs=[VMEM] * 3,
        out_shape=[
            pltpu.VMEM((outs, nbox, points), BF16),
            pltpu.VMEM((outs, nbox, points), BF16),
            pltpu.VMEM((nbox, points), F32),
        ],
        scratch_shapes=[
            pltpu.SMEM(signs.shape, signs.dtype),
            pltpu.VMEM((count, nbox, points), BF16),
            pltpu.VMEM((outs * group, count * group), BF16),
            pltpu.SemaphoreType.DMA((2, nbox // block + 1)),
        ],
        compiler_params=pltpu.CompilerParams(vmem_limit_bytes=12 * 2**20),
        cost_estimate=pl.CostEstimate(
            flops=2 * outs * count * group * nbox * points,
            bytes_accessed=nbox * points * 2 * count,
            transcendentals=0,
        ),
        name="encode",
    )(far(signs), far(incident), far(adjoint))


def weigh_kernel(block, first, adj, enc, _, adj_in, part_in, adjv, part, sems):
    nbox = enc.shape[1]
    steps = nbox // block

    def copy(i):
        rows = pl.ds(pl.multiple_of(i * block, ROWS), block)
        return pltpu.make_async_copy(adj.at[0, :, rows, :], adjv.at[:, rows, :], sems.at[i])

    for i in range(first, steps):
        copy(i).start()

    def step(i, carry):
        copy(i).wait()
        rows = pl.ds(pl.multiple_of(i * block, ROWS), block)
        part[rows, :] = jnp.sum(adjv[:, rows, :].astype(F32) * enc[:, rows, :].astype(F32), axis=0)
        return carry

    lax.fori_loop(first, steps, step, 0)


def weigh(adjoint, enc, adj, part, weighed, after, block=32):
    outs, nbox, points = enc.shape
    return pl.pallas_call(
        functools.partial(weigh_kernel, block, weighed // block),
        in_specs=[HBM] + [VMEM] * 4,
        out_specs=[VMEM, VMEM],
        out_shape=[pltpu.VMEM((outs, nbox, points), BF16), pltpu.VMEM((nbox, points), F32)],
        input_output_aliases={3: 0, 4: 1},
        scratch_shapes=[pltpu.SemaphoreType.DMA((nbox // block,))],
        compiler_params=pltpu.CompilerParams(vmem_limit_bytes=8 * 2**20),
        cost_estimate=pl.CostEstimate(flops=1, bytes_accessed=1, transcendentals=0),
        name="weigh",
    )(far(adjoint), near(enc), near(after), near(adj), near(part))


def add_kernel(jobs, *refs):
    for out, place, terms in jobs:
        value = None
        for ref, slot, first, extent in terms:
            ref = refs[ref]
            x = ref[first:first + extent, :] if slot is None else ref[slot, first:first + extent, :]
            x = x.astype(F32)
            value = x if value is None else value + x
        refs[out][place:place + value.shape[0], :] = value.astype(refs[out].dtype)


def add(jobs, operands, shapes):
    return pl.pallas_call(
        functools.partial(add_kernel, jobs),
        in_specs=[VMEM] * len(operands),
        out_specs=[VMEM] * len(shapes),
        out_shape=shapes,
        compiler_params=pltpu.CompilerParams(vmem_limit_bytes=4 * 2**20),
        name="add",
    )(*map(near, operands))


def leaving(ready, scattered, segments, sems):
    copies, row = [], 0
    for i, (first, size) in enumerate(segments):
        copies.append(
            pltpu.make_async_copy(
                ready.at[:, row:row + size, :], scattered.at[0, :, first:first + size, :], sems.at[i]
            )
        )
        row += size
    return copies


def stage_kernel(axis, count, mine, blocks, edges_at, phases, layout, *refs):
    named, at = {}, 0
    for name, number in layout:
        named[name] = refs[at] if number is None else refs[at:at + number]
        at += 1 if number is None else number
    offsets, mats, expand = named["offsets"], named["mats"], named["expand"]
    adj, part = named["adj"], named["part"]
    padded, ready = named["padded"], named["ready"]
    held, terms = refs[at:]
    outs, nbox, points = adj.shape
    operators, depth, width = mats.shape
    share = points // count
    halves, _, _, lanes = padded.shape
    me = lax.axis_index(axis)
    starts = [pl.multiple_of((me ^ m) * share, share) for m in range(count)]

    def fill(place, extent, values):
        for h in range(halves):
            padded[h, :, place + ROWS:place + ROWS + extent, :] = values[
                :, :, h * lanes:(h + 1) * lanes
            ].astype(F32)

    if mine:
        enc, proj, contrasts = named["enc"], named["proj"], named["pieces"]
        weights = jnp.concatenate([proj[pl.ds(s, share), :] for s in starts], axis=0)
        for runs in mine:
            source = [
                jnp.concatenate(
                    [
                        contrast[row:row + size, :][None]
                        * enc[:, first:first + size, pl.ds(start, share)]
                        for contrast, start in zip(contrasts, starts)
                    ],
                    axis=2,
                )
                for first, row, size in runs
            ]
            total = sum(size for _, _, size in runs)
            source = jnp.concatenate(source, axis=1).reshape(outs * total, points)
            coeffs = jnp.dot(source, weights, preferred_element_type=F32).astype(BF16)
            coeffs = coeffs.reshape(outs, total, width)
            done = 0
            for first, _, size in runs:
                fill(first, size, coeffs[:, done:done + size, :])
                done += size
    for edge, place in zip(named.get("edges", ()), edges_at):
        for h in range(halves):
            edge[:, :, h * lanes:(h + 1) * lanes] = padded[
                h, :, place + ROWS:place + 2 * ROWS, :
            ].astype(BF16)
    if "low" in named:
        fill(-ROWS, ROWS, named["low"][...])
        fill(nbox, ROWS, named["high"][...])

    def translated(first, size):
        moved = [
            padded[h, :, pl.ds(first + ROWS + offsets[t], size), :]
            .astype(BF16)
            .reshape(outs * size, lanes)
            for t in range(operators)
            for h in range(halves)
        ]
        return jnp.dot(
            jnp.concatenate(moved, axis=1),
            mats[...].reshape(operators * depth, width),
            preferred_element_type=F32,
        ).astype(BF16)

    def finish(i, local):
        first, size, row = blocks[i]
        field = jnp.dot(local, expand[...], preferred_element_type=F32)
        field = field.reshape(outs, size, points)
        ready[:, row:row + size, :] = field.astype(BF16)
        terms[0:size, :] = part[first:first + size, :] + jnp.sum(
            adj[:, first:first + size, :].astype(F32) * field, axis=0
        )
        named["own"][row:row + size, :] = terms[0:size, pl.ds(starts[0], share)]
        for phase, members in enumerate(phases):
            for slot, m in enumerate(members):
                named["sent"][phase][slot, row:row + size, :] = terms[
                    0:size, pl.ds(starts[m], share)
                ].astype(BF16)

    rows_of = [outs * size for _, size, _ in blocks]
    held[0, 0:rows_of[0], :] = translated(*blocks[0][:2])
    for i in range(len(blocks)):
        if i + 1 < len(blocks):
            following = translated(*blocks[i + 1][:2])
        finish(i, held[i % 2, 0:rows_of[i], :])
        if i + 1 < len(blocks):
            held[(i + 1) % 2, 0:rows_of[i + 1], :] = following


def stage(axis, count, mine, blocks, edges_at, phases, inputs, state, weight=1.0):
    outs, nbox, points = inputs["adj"].shape
    depth, width = inputs["mats"].shape[1:]
    share = points // count
    lanes = min(128, width)
    placed, rows = [], 0
    for first, size in blocks:
        placed.append((first, size, rows))
        rows += size
    most = max(size for _, size in blocks)

    layout, operands, specs = [], [], []
    for name, value in inputs.items():
        many = isinstance(value, (list, tuple))
        layout.append((name, len(value) if many else None))
        for x in value if many else [value]:
            operands.append(x if name == "offsets" else near(x))
            specs.append(SMEM if name == "offsets" else VMEM)
    aliases = {}
    if state is not None:
        layout.append(("padded_in", None))
        aliases = {len(operands): 0}
        operands.append(near(state))
        specs.append(VMEM)

    layout += [("padded", None), ("ready", None), ("own", None), ("sent", len(phases))]
    out_shape = [
        pltpu.VMEM((width // lanes, outs, nbox + 2 * ROWS, lanes), F32),
        pltpu.VMEM((outs, rows, points), BF16),
        pltpu.VMEM((rows, share), F32),
    ]
    out_shape += [pltpu.VMEM((len(members), rows, share), BF16) for members in phases]
    out_specs = [VMEM] * 3 + [VMEM] * len(phases)
    if edges_at:
        layout.append(("edges", len(edges_at)))
        out_shape += [pltpu.VMEM((outs, ROWS, width), BF16)] * len(edges_at)
        out_specs += [VMEM] * len(edges_at)
    made = sum(size for runs in mine for _, _, size in runs)
    result = pl.pallas_call(
        functools.partial(stage_kernel, axis, count, mine, placed, edges_at, phases, layout),
        in_specs=specs,
        out_specs=out_specs,
        out_shape=out_shape,
        input_output_aliases=aliases,
        scratch_shapes=[
            pltpu.VMEM((2, outs * most, width), BF16),
            pltpu.VMEM((most, points), F32),
        ],
        compiler_params=pltpu.CompilerParams(vmem_limit_bytes=16 * 2**20),
        cost_estimate=pl.CostEstimate(
            flops=int(
                weight * 2 * outs * width
                * (made * points + rows * (inputs["mats"].shape[0] * depth + points))
            ),
            bytes_accessed=int(weight * rows * points * 2 * outs),
            transcendentals=0,
        ),
        name="stage",
    )(*operands)
    padded, ready, own = result[:3]
    return padded, (ready, joined(blocks)), own, result[3:3 + len(phases)], result[3 + len(phases):]


def joined(blocks):
    segments = []
    for first, size in blocks:
        if segments and sum(segments[-1]) == first:
            segments[-1] = (segments[-1][0], segments[-1][1] + size)
        else:
            segments.append((first, size))
    return segments


def flush_kernel(segments, *refs):
    scattered, sems = refs[-2:]
    copies = []
    for ready, held in zip(refs, segments):
        copies += leaving(ready, scattered, held, sems.at[pl.ds(len(copies), len(held))])
    for copy in copies:
        copy.start()
    for copy in copies:
        copy.wait()


def flush(fields, nbox, after):
    outs, _, points = fields[0][0].shape
    segments = [held for _, held in fields]
    return pl.pallas_call(
        functools.partial(flush_kernel, segments),
        in_specs=[VMEM] * (len(fields) + 1),
        out_specs=HBM,
        out_shape=jax.ShapeDtypeStruct((1, outs, nbox, points), BF16),
        scratch_shapes=[pltpu.SemaphoreType.DMA((sum(map(len, segments)),))],
        compiler_params=pltpu.CompilerParams(vmem_limit_bytes=4 * 2**20),
        cost_estimate=pl.CostEstimate(flops=1, bytes_accessed=1, transcendentals=0),
        name="flush",
    )(*[near(ready) for ready, _ in fields], near(after))


def cut_up(first, extent, parts):
    tiles = extent // ROWS
    sizes = [ROWS * (tiles // parts + (i < tiles % parts)) for i in range(parts)]
    return [(first + sum(sizes[:i]), size) for i, size in enumerate(sizes) if size]


def exchange(x, axis, m, count):
    return lax.ppermute(x, axis, [(i, i ^ m) for i in range(count)])


def gather_pieces(pieces, axis, count):
    for m in sorted(range(1, count), key=lambda m: (bin(m).count("1"), -m)):
        if m not in pieces:
            pieces[m] = exchange(pieces[m & (m - 1)], axis, m & -m, count)
    return [pieces[m] for m in range(count)]


def hypercube(count):
    bits = [1 << k for k in range(count.bit_length() - 1)]
    return [[m for m in reversed(range(count)) if m & -m == b] for b in bits]


def folded(members, sent, got, kept):
    for s, m in enumerate(members):
        if m & (m - 1):
            kept[m & (m - 1)] = (kept[m & (m - 1)].astype(F32) + got[s].astype(F32)).astype(BF16)
    return kept


def scatter_steps(sent, axis, count):
    phases = hypercube(count)
    kept = {m: sent[p][s] for p, members in enumerate(phases) for s, m in enumerate(members)}
    final = []
    for p, members in enumerate(phases):
        whole = sent[p] if p == 0 else jnp.stack([kept[m] for m in members])
        got = exchange(whole, axis, 1 << p, count)
        kept = folded(members, sent, got, kept)
        final.append((got, len(members) - 1))
    return final


def first_step(sent, after, axis, count, own=None, got=()):
    phases = hypercube(count)
    came = exchange(sent[0], axis, 1, count)
    rows, share = sent[0].shape[1:]
    operands = [came] + list(sent[1:]) + list(after)
    jobs, shapes, order = [], [], []
    outs = len(operands) + (0 if own is None else 1 + len(got))
    for p, members in enumerate(phases[1:]):
        for s, m in enumerate(members):
            terms = [(1 + p, s, 0, rows)]
            if m + 1 in phases[0]:
                terms.append((0, phases[0].index(m + 1), 0, rows))
            jobs.append((outs + len(order), 0, terms))
            shapes.append(pltpu.VMEM((rows, share), BF16))
            order.append(m)
    if own is not None:
        terms = [(len(operands), None, 0, own.shape[0])]
        terms += [(len(operands) + 1 + i, slot, 0, own.shape[0]) for i, (_, slot) in enumerate(got)]
        jobs.append((outs + len(order), 0, terms))
        shapes.append(pltpu.VMEM(own.shape, F32))
        operands += [own] + [x for x, _ in got]
    result = add(jobs, operands, shapes)
    return (came, dict(zip(order, result))), result[len(order):]


def scatter_last(begun, axis, count):
    came, kept = begun
    phases = hypercube(count)
    final = [(came, len(phases[0]) - 1)]
    for p, members in enumerate(phases):
        if p:
            got = exchange(jnp.stack([kept[m] for m in members]), axis, 1 << p, count)
            kept = folded(members, None, got, kept)
            final.append((got, len(members) - 1))
    return final


def scatter_direct(sent, axis, count):
    return [(exchange(x, axis, m, count), 0) for m, x in enumerate(sent, start=1)]


def on_device(groups, tiles, contrast, incident, signs, adjoint, proj, mats, offsets, expand):
    nbox = contrast.shape[0]
    half = nbox // 32 * 15
    cut, last = half + ROWS, nbox - ROWS
    third = nbox // 32 * 27
    upward = [(i, i + 1) for i in range(tiles - 1)]
    downward = [(i + 1, i) for i in range(tiles - 1)]

    contrast_a, contrast_b = split(contrast, [[(0, cut), (last, ROWS)], [(cut, last - cut)]])
    far_side = groups // 2
    first = exchange(contrast_a, "group", 1, groups)
    top = exchange(contrast_a, "group", far_side, groups)
    weighed = nbox // 2
    enc, adj, part = encode(signs, incident, adjoint, weighed)
    top, first, enc = lax.optimization_barrier((top, first, enc))
    pieces_a = gather_pieces({0: contrast_a, 1: first, far_side: top}, "group", groups)
    adj, part = weigh(adjoint, enc, adj, part, weighed, top)
    part, contrast_b = lax.optimization_barrier((part, contrast_b))
    pieces_b = [contrast_b] + [exchange(contrast_b, "group", m, groups) for m in range(1, groups)]

    common = dict(offsets=offsets, mats=mats, expand=expand, adj=adj, part=part)
    mine = [[(first, first, size)] for first, size in cut_up(0, cut, 2)]
    mine[-1].append((last, cut, ROWS))
    state, field_a, own_a, sent_a, edges = stage(
        "group", groups, mine, cut_up(ROWS, half - ROWS, 3), (0, last),
        hypercube(groups), common | dict(enc=enc, proj=proj, pieces=pieces_a), None, weight=0.0,
    )
    high = lax.ppermute(edges[0], "tile", downward)
    low = lax.ppermute(edges[1], "tile", upward)

    mine = [[(first, first - cut, size)] for first, size in cut_up(cut, last - cut, 2)]
    state, field_b, own_b, sent_b, _ = stage(
        "group", groups, mine, cut_up(half, third - half, 2), (),
        hypercube(groups), common | dict(enc=enc, proj=proj, pieces=pieces_b), state, weight=1.0,
    )
    got_a = scatter_steps(sent_a, "group", groups)
    _, field_c, own_c, sent_c, _ = stage(
        "group", groups, [], cut_up(third, nbox - third, 2) + [(0, ROWS)], (),
        hypercube(groups), common | dict(low=low, high=high), state, weight=1.0,
    )
    share = own_a.shape[1]
    rows_a, rows_b, rows_c = half - ROWS, third - half, nbox - third
    begun_b, _ = first_step(sent_b, [sent_c[0]], "group", groups)
    got_b = scatter_last(begun_b, "group", groups)
    begun_c, (done_a,) = first_step(sent_c, [begun_b[1][2]] if groups > 2 else [], "group", groups, own_a, got_a)
    got_c = scatter_last(begun_c, "group", groups)

    operands = [done_a, own_b] + [x for x, _ in got_b] + [own_c] + [x for x, _ in got_c]
    at_c = 2 + len(got_b)
    out = len(operands)
    pick_b = [(1, None)] + [(2 + i, slot) for i, (_, slot) in enumerate(got_b)]
    pick_c = [(at_c, None)] + [(at_c + 1 + i, slot) for i, (_, slot) in enumerate(got_c)]
    jobs = [
        (out, 0, [(ref, slot, rows_c, ROWS) for ref, slot in pick_c]),
        (out, ROWS, [(0, None, 0, rows_a)]),
        (out, half, [(ref, slot, 0, rows_b) for ref, slot in pick_b]),
        (out, third, [(ref, slot, 0, rows_c) for ref, slot in pick_c]),
    ]
    (gradient,) = add(jobs, operands, [jax.ShapeDtypeStruct((nbox, share), F32)])
    scattered = flush([field_a, field_b, field_c], nbox, got_c[0][0])
    return scattered, gradient


def solution(mesh):
    in_specs = (
        P("tile", "group"),
        P("group", None, "tile", None),
        P("group", None, None),
        P("group", None, "tile", None),
        P(),
        P(),
        P(),
        P(),
    )
    out_specs = (P("group", None, "tile", None), P("tile", "group"))
    return jax.shard_map(
        functools.partial(on_device, mesh.shape["group"], mesh.shape["tile"]),
        mesh=mesh,
        in_specs=in_specs,
        out_specs=out_specs,
        check_vma=False,
    )
```

```python
import functools

import jax
import jax.numpy as jnp
from jax import lax
from jax.experimental import pallas as pl
from jax.experimental.pallas import tpu as pltpu
from jax.sharding import PartitionSpec as P

F32 = jnp.float32
BF16 = jnp.bfloat16
ROWS = 16
VMEM = pl.BlockSpec(memory_space=pltpu.VMEM)
SMEM = pl.BlockSpec(memory_space=pltpu.SMEM)
ANY = pl.BlockSpec(memory_space=pl.ANY)
HBM = pl.BlockSpec(memory_space=pltpu.HBM)


def near(x):
    return pltpu.with_memory_space_constraint(x, pltpu.VMEM)


def far(x):
    return pltpu.with_memory_space_constraint(x, pltpu.HBM)


def split_kernel(runs, whole, *refs):
    outs, sems = refs[:-1], refs[-1]
    copies = [
        pltpu.make_async_copy(
            whole.at[first:first + extent, :], outs[to].at[row:row + extent, :], sems.at[i]
        )
        for i, (to, row, first, extent) in enumerate(runs)
    ]
    for copy in copies:
        copy.start()
    for copy in copies:
        copy.wait()


def split(x, parts):
    runs, shapes = [], []
    for to, part in enumerate(parts):
        row = 0
        for first, extent in part:
            runs.append((to, row, first, extent))
            row += extent
        shapes.append(pltpu.VMEM((row, x.shape[1]), x.dtype))
    return pl.pallas_call(
        functools.partial(split_kernel, runs),
        in_specs=[HBM],
        out_specs=[VMEM] * len(parts),
        out_shape=shapes,
        scratch_shapes=[pltpu.SemaphoreType.DMA((len(runs),))],
        compiler_params=pltpu.CompilerParams(vmem_limit_bytes=4 * 2**20),
        name="split",
    )(far(x))


def encode_kernel(block, group, weighed, signs_in, inc, adj, enc, adjv, part, signs, incv, mix, sems):
    count, nbox, points = incv.shape
    outs = enc.shape[0]
    size = count * group
    steps = nbox // block

    def copies(i):
        rows = pl.ds(pl.multiple_of(i * block, ROWS), block)
        inc_copy = pltpu.make_async_copy(inc.at[0, :, rows, :], incv.at[:, rows, :], sems.at[0, i])
        adj_copy = pltpu.make_async_copy(adj.at[0, :, rows, :], adjv.at[:, rows, :], sems.at[1, i])
        return inc_copy, adj_copy

    signs_copy = pltpu.make_async_copy(signs_in, signs, sems.at[0, steps])
    signs_copy.start()
    for i in range(steps):
        inc_copy, adj_copy = copies(i)
        inc_copy.start()
        if i < weighed:
            adj_copy.start()
    signs_copy.wait()

    r = lax.broadcasted_iota(jnp.int32, (group, size), 0)
    c = lax.broadcasted_iota(jnp.int32, (group, size), 1)
    diagonal = (c % group) == r
    for e in range(outs):
        value = jnp.zeros((group, size), F32)
        for s in range(count):
            value = jnp.where(c // group == s, signs[0, e, s].astype(F32), value)
        mix[e * group:(e + 1) * group, :] = jnp.where(diagonal, value, 0.0).astype(BF16)

    def step(i, carry, weigh):
        inc_copy, adj_copy = copies(i)
        inc_copy.wait()
        if weigh:
            adj_copy.wait()
        for j in range(block // group):
            rows = pl.ds(pl.multiple_of(i * block + j * group, ROWS), group)
            x = incv[:, rows, :].reshape(size, points)
            encoded = jnp.dot(mix[...], x, preferred_element_type=F32).astype(BF16)
            encoded = encoded.reshape(outs, group, points)
            enc[:, rows, :] = encoded
            if weigh:
                part[rows, :] = jnp.sum(adjv[:, rows, :].astype(F32) * encoded.astype(F32), axis=0)
        return carry

    lax.fori_loop(0, weighed, functools.partial(step, weigh=True), 0)
    lax.fori_loop(weighed, steps, functools.partial(step, weigh=False), 0)


def encode(signs, incident, adjoint, weighed, block=32):
    _, count, nbox, points = incident.shape
    outs = adjoint.shape[1]
    group = 256 // count
    return pl.pallas_call(
        functools.partial(encode_kernel, block, group, weighed // block),
        in_specs=[HBM, HBM, HBM],
        out_specs=[VMEM] * 3,
        out_shape=[
            pltpu.VMEM((outs, nbox, points), BF16),
            pltpu.VMEM((outs, nbox, points), BF16),
            pltpu.VMEM((nbox, points), F32),
        ],
        scratch_shapes=[
            pltpu.SMEM(signs.shape, signs.dtype),
            pltpu.VMEM((count, nbox, points), BF16),
            pltpu.VMEM((outs * group, count * group), BF16),
            pltpu.SemaphoreType.DMA((2, nbox // block + 1)),
        ],
        compiler_params=pltpu.CompilerParams(vmem_limit_bytes=12 * 2**20),
        cost_estimate=pl.CostEstimate(
            flops=2 * outs * count * group * nbox * points,
            bytes_accessed=nbox * points * 2 * count,
            transcendentals=0,
        ),
        name="encode",
    )(far(signs), far(incident), far(adjoint))


def weigh_kernel(block, first, adj, enc, _, adj_in, part_in, adjv, part, sems):
    nbox = enc.shape[1]
    steps = nbox // block

    def copy(i):
        rows = pl.ds(pl.multiple_of(i * block, ROWS), block)
        return pltpu.make_async_copy(adj.at[0, :, rows, :], adjv.at[:, rows, :], sems.at[i])

    for i in range(first, steps):
        copy(i).start()

    def step(i, carry):
        copy(i).wait()
        rows = pl.ds(pl.multiple_of(i * block, ROWS), block)
        part[rows, :] = jnp.sum(adjv[:, rows, :].astype(F32) * enc[:, rows, :].astype(F32), axis=0)
        return carry

    lax.fori_loop(first, steps, step, 0)


def weigh(adjoint, enc, adj, part, weighed, after, block=32):
    outs, nbox, points = enc.shape
    return pl.pallas_call(
        functools.partial(weigh_kernel, block, weighed // block),
        in_specs=[HBM] + [VMEM] * 4,
        out_specs=[VMEM, VMEM],
        out_shape=[pltpu.VMEM((outs, nbox, points), BF16), pltpu.VMEM((nbox, points), F32)],
        input_output_aliases={3: 0, 4: 1},
        scratch_shapes=[pltpu.SemaphoreType.DMA((nbox // block,))],
        compiler_params=pltpu.CompilerParams(vmem_limit_bytes=8 * 2**20),
        cost_estimate=pl.CostEstimate(flops=1, bytes_accessed=1, transcendentals=0),
        name="weigh",
    )(far(adjoint), near(enc), near(after), near(adj), near(part))


def add_kernel(jobs, *refs):
    for out, place, terms in jobs:
        value = None
        for ref, slot, first, extent in terms:
            ref = refs[ref]
            x = ref[first:first + extent, :] if slot is None else ref[slot, first:first + extent, :]
            x = x.astype(F32)
            value = x if value is None else value + x
        refs[out][place:place + value.shape[0], :] = value.astype(refs[out].dtype)


def add(jobs, operands, shapes):
    return pl.pallas_call(
        functools.partial(add_kernel, jobs),
        in_specs=[VMEM] * len(operands),
        out_specs=[VMEM] * len(shapes),
        out_shape=shapes,
        compiler_params=pltpu.CompilerParams(vmem_limit_bytes=4 * 2**20),
        name="add",
    )(*map(near, operands))


def leaving(ready, scattered, segments, sems):
    copies, row = [], 0
    for i, (first, size) in enumerate(segments):
        copies.append(
            pltpu.make_async_copy(
                ready.at[:, row:row + size, :], scattered.at[0, :, first:first + size, :], sems.at[i]
            )
        )
        row += size
    return copies


def stage_kernel(axis, count, mine, blocks, edges_at, phases, layout, *refs):
    named, at = {}, 0
    for name, number in layout:
        named[name] = refs[at] if number is None else refs[at:at + number]
        at += 1 if number is None else number
    offsets, mats, expand = named["offsets"], named["mats"], named["expand"]
    adj, part = named["adj"], named["part"]
    padded, ready = named["padded"], named["ready"]
    held, terms = refs[at:]
    outs, nbox, points = adj.shape
    operators, depth, width = mats.shape
    share = points // count
    halves, _, _, lanes = padded.shape
    me = lax.axis_index(axis)
    starts = [pl.multiple_of((me ^ m) * share, share) for m in range(count)]

    def fill(place, extent, values):
        for h in range(halves):
            padded[h, :, place + ROWS:place + ROWS + extent, :] = values[
                :, :, h * lanes:(h + 1) * lanes
            ].astype(F32)

    if mine:
        enc, proj, contrasts = named["enc"], named["proj"], named["pieces"]
        weights = jnp.concatenate([proj[pl.ds(s, share), :] for s in starts], axis=0)
        for runs in mine:
            source = [
                jnp.concatenate(
                    [
                        contrast[row:row + size, :][None]
                        * enc[:, first:first + size, pl.ds(start, share)]
                        for contrast, start in zip(contrasts, starts)
                    ],
                    axis=2,
                )
                for first, row, size in runs
            ]
            total = sum(size for _, _, size in runs)
            source = jnp.concatenate(source, axis=1).reshape(outs * total, points)
            coeffs = jnp.dot(source, weights, preferred_element_type=F32).astype(BF16)
            coeffs = coeffs.reshape(outs, total, width)
            done = 0
            for first, _, size in runs:
                fill(first, size, coeffs[:, done:done + size, :])
                done += size
    for edge, place in zip(named.get("edges", ()), edges_at):
        for h in range(halves):
            edge[:, :, h * lanes:(h + 1) * lanes] = padded[
                h, :, place + ROWS:place + 2 * ROWS, :
            ].astype(BF16)
    if "low" in named:
        fill(-ROWS, ROWS, named["low"][...])
        fill(nbox, ROWS, named["high"][...])

    def translated(first, size):
        moved = [
            padded[h, :, pl.ds(first + ROWS + offsets[t], size), :]
            .astype(BF16)
            .reshape(outs * size, lanes)
            for t in range(operators)
            for h in range(halves)
        ]
        return jnp.dot(
            jnp.concatenate(moved, axis=1),
            mats[...].reshape(operators * depth, width),
            preferred_element_type=F32,
        ).astype(BF16)

    def finish(i, local):
        first, size, row = blocks[i]
        field = jnp.dot(local, expand[...], preferred_element_type=F32)
        field = field.reshape(outs, size, points)
        ready[:, row:row + size, :] = field.astype(BF16)
        terms[0:size, :] = part[first:first + size, :] + jnp.sum(
            adj[:, first:first + size, :].astype(F32) * field, axis=0
        )
        named["own"][row:row + size, :] = terms[0:size, pl.ds(starts[0], share)]
        for phase, members in enumerate(phases):
            for slot, m in enumerate(members):
                named["sent"][phase][slot, row:row + size, :] = terms[
                    0:size, pl.ds(starts[m], share)
                ].astype(BF16)

    rows_of = [outs * size for _, size, _ in blocks]
    held[0, 0:rows_of[0], :] = translated(*blocks[0][:2])
    for i in range(len(blocks)):
        if i + 1 < len(blocks):
            following = translated(*blocks[i + 1][:2])
        finish(i, held[i % 2, 0:rows_of[i], :])
        if i + 1 < len(blocks):
            held[(i + 1) % 2, 0:rows_of[i + 1], :] = following


def stage(axis, count, mine, blocks, edges_at, phases, inputs, state, weight=1.0):
    outs, nbox, points = inputs["adj"].shape
    depth, width = inputs["mats"].shape[1:]
    share = points // count
    lanes = min(128, width)
    placed, rows = [], 0
    for first, size in blocks:
        placed.append((first, size, rows))
        rows += size
    most = max(size for _, size in blocks)

    layout, operands, specs = [], [], []
    for name, value in inputs.items():
        many = isinstance(value, (list, tuple))
        layout.append((name, len(value) if many else None))
        for x in value if many else [value]:
            operands.append(x if name == "offsets" else near(x))
            specs.append(SMEM if name == "offsets" else VMEM)
    aliases = {}
    if state is not None:
        layout.append(("padded_in", None))
        aliases = {len(operands): 0}
        operands.append(near(state))
        specs.append(VMEM)

    layout += [("padded", None), ("ready", None), ("own", None), ("sent", len(phases))]
    out_shape = [
        pltpu.VMEM((width // lanes, outs, nbox + 2 * ROWS, lanes), F32),
        pltpu.VMEM((outs, rows, points), BF16),
        pltpu.VMEM((rows, share), F32),
    ]
    out_shape += [pltpu.VMEM((len(members), rows, share), BF16) for members in phases]
    out_specs = [VMEM] * 3 + [VMEM] * len(phases)
    if edges_at:
        layout.append(("edges", len(edges_at)))
        out_shape += [pltpu.VMEM((outs, ROWS, width), BF16)] * len(edges_at)
        out_specs += [VMEM] * len(edges_at)
    made = sum(size for runs in mine for _, _, size in runs)
    result = pl.pallas_call(
        functools.partial(stage_kernel, axis, count, mine, placed, edges_at, phases, layout),
        in_specs=specs,
        out_specs=out_specs,
        out_shape=out_shape,
        input_output_aliases=aliases,
        scratch_shapes=[
            pltpu.VMEM((2, outs * most, width), BF16),
            pltpu.VMEM((most, points), F32),
        ],
        compiler_params=pltpu.CompilerParams(vmem_limit_bytes=16 * 2**20),
        cost_estimate=pl.CostEstimate(
            flops=int(
                weight * 2 * outs * width
                * (made * points + rows * (inputs["mats"].shape[0] * depth + points))
            ),
            bytes_accessed=int(weight * rows * points * 2 * outs),
            transcendentals=0,
        ),
        name="stage",
    )(*operands)
    padded, ready, own = result[:3]
    return padded, (ready, joined(blocks)), own, result[3:3 + len(phases)], result[3 + len(phases):]


def joined(blocks):
    segments = []
    for first, size in blocks:
        if segments and sum(segments[-1]) == first:
            segments[-1] = (segments[-1][0], segments[-1][1] + size)
        else:
            segments.append((first, size))
    return segments


def flush_kernel(segments, *refs):
    scattered, sems = refs[-2:]
    copies = []
    for ready, held in zip(refs, segments):
        copies += leaving(ready, scattered, held, sems.at[pl.ds(len(copies), len(held))])
    for copy in copies:
        copy.start()
    for copy in copies:
        copy.wait()


def flush(fields, nbox, after):
    outs, _, points = fields[0][0].shape
    segments = [held for _, held in fields]
    return pl.pallas_call(
        functools.partial(flush_kernel, segments),
        in_specs=[VMEM] * (len(fields) + 1),
        out_specs=HBM,
        out_shape=jax.ShapeDtypeStruct((1, outs, nbox, points), BF16),
        scratch_shapes=[pltpu.SemaphoreType.DMA((sum(map(len, segments)),))],
        compiler_params=pltpu.CompilerParams(vmem_limit_bytes=4 * 2**20),
        cost_estimate=pl.CostEstimate(flops=1, bytes_accessed=1, transcendentals=0),
        name="flush",
    )(*[near(ready) for ready, _ in fields], near(after))


def cut_up(first, extent, parts):
    tiles = extent // ROWS
    sizes = [ROWS * (tiles // parts + (i < tiles % parts)) for i in range(parts)]
    return [(first + sum(sizes[:i]), size) for i, size in enumerate(sizes) if size]


def exchange(x, axis, m, count):
    return lax.ppermute(x, axis, [(i, i ^ m) for i in range(count)])


def gather_pieces(pieces, axis, count):
    for m in sorted(range(1, count), key=lambda m: (bin(m).count("1"), -m)):
        if m not in pieces:
            pieces[m] = exchange(pieces[m & (m - 1)], axis, m & -m, count)
    return [pieces[m] for m in range(count)]


def hypercube(count):
    bits = [1 << k for k in range(count.bit_length() - 1)]
    return [[m for m in reversed(range(count)) if m & -m == b] for b in bits]


def folded(members, sent, got, kept):
    for s, m in enumerate(members):
        if m & (m - 1):
            kept[m & (m - 1)] = (kept[m & (m - 1)].astype(F32) + got[s].astype(F32)).astype(BF16)
    return kept


def scatter_steps(sent, axis, count):
    phases = hypercube(count)
    kept = {m: sent[p][s] for p, members in enumerate(phases) for s, m in enumerate(members)}
    final = []
    for p, members in enumerate(phases):
        whole = sent[p] if p == 0 else jnp.stack([kept[m] for m in members])
        got = exchange(whole, axis, 1 << p, count)
        kept = folded(members, sent, got, kept)
        final.append((got, len(members) - 1))
    return final


def first_step(sent, after, axis, count, own=None, got=()):
    phases = hypercube(count)
    came = exchange(sent[0], axis, 1, count)
    rows, share = sent[0].shape[1:]
    operands = [came] + list(sent[1:]) + list(after)
    jobs, shapes, order = [], [], []
    outs = len(operands) + (0 if own is None else 1 + len(got))
    for p, members in enumerate(phases[1:]):
        for s, m in enumerate(members):
            terms = [(1 + p, s, 0, rows)]
            if m + 1 in phases[0]:
                terms.append((0, phases[0].index(m + 1), 0, rows))
            jobs.append((outs + len(order), 0, terms))
            shapes.append(pltpu.VMEM((rows, share), BF16))
            order.append(m)
    if own is not None:
        terms = [(len(operands), None, 0, own.shape[0])]
        terms += [(len(operands) + 1 + i, slot, 0, own.shape[0]) for i, (_, slot) in enumerate(got)]
        jobs.append((outs + len(order), 0, terms))
        shapes.append(pltpu.VMEM(own.shape, F32))
        operands += [own] + [x for x, _ in got]
    result = add(jobs, operands, shapes)
    return (came, dict(zip(order, result))), result[len(order):]


def scatter_last(begun, axis, count):
    came, kept = begun
    phases = hypercube(count)
    final = [(came, len(phases[0]) - 1)]
    for p, members in enumerate(phases):
        if p:
            got = exchange(jnp.stack([kept[m] for m in members]), axis, 1 << p, count)
            kept = folded(members, None, got, kept)
            final.append((got, len(members) - 1))
    return final


def scatter_direct(sent, axis, count):
    return [(exchange(x, axis, m, count), 0) for m, x in enumerate(sent, start=1)]


def on_device(groups, tiles, contrast, incident, signs, adjoint, proj, mats, offsets, expand):
    nbox = contrast.shape[0]
    half = nbox // 32 * 15
    cut, last = half + ROWS, nbox - ROWS
    third = nbox // 32 * 27
    upward = [(i, i + 1) for i in range(tiles - 1)]
    downward = [(i + 1, i) for i in range(tiles - 1)]

    contrast_a, contrast_b = split(contrast, [[(0, cut), (last, ROWS)], [(cut, last - cut)]])
    far_side = groups // 2
    first = exchange(contrast_a, "group", 1, groups)
    top = exchange(contrast_a, "group", far_side, groups)
    weighed = nbox // 8 * 5
    enc, adj, part = encode(signs, incident, adjoint, weighed)
    top, first, enc = lax.optimization_barrier((top, first, enc))
    pieces_a = gather_pieces({0: contrast_a, 1: first, far_side: top}, "group", groups)
    adj, part = weigh(adjoint, enc, adj, part, weighed, top)
    part, contrast_b = lax.optimization_barrier((part, contrast_b))
    pieces_b = [contrast_b] + [exchange(contrast_b, "group", m, groups) for m in range(1, groups)]

    common = dict(offsets=offsets, mats=mats, expand=expand, adj=adj, part=part)
    mine = [[(first, first, size)] for first, size in cut_up(0, cut, 2)]
    mine[-1].append((last, cut, ROWS))
    state, field_a, own_a, sent_a, edges = stage(
        "group", groups, mine, cut_up(ROWS, half - ROWS, 3), (0, last),
        hypercube(groups), common | dict(enc=enc, proj=proj, pieces=pieces_a), None, weight=0.0,
    )
    high = lax.ppermute(edges[0], "tile", downward)
    low = lax.ppermute(edges[1], "tile", upward)

    mine = [[(first, first - cut, size)] for first, size in cut_up(cut, last - cut, 2)]
    state, field_b, own_b, sent_b, _ = stage(
        "group", groups, mine, cut_up(half, third - half, 2), (),
        hypercube(groups), common | dict(enc=enc, proj=proj, pieces=pieces_b), state, weight=1.0,
    )
    got_a = scatter_steps(sent_a, "group", groups)
    _, field_c, own_c, sent_c, _ = stage(
        "group", groups, [], cut_up(third, nbox - third, 2) + [(0, ROWS)], (),
        hypercube(groups), common | dict(low=low, high=high), state, weight=1.0,
    )
    share = own_a.shape[1]
    rows_a, rows_b, rows_c = half - ROWS, third - half, nbox - third
    begun_b, _ = first_step(sent_b, [sent_c[0]], "group", groups)
    got_b = scatter_last(begun_b, "group", groups)
    begun_c, (done_a,) = first_step(sent_c, [begun_b[1][2]] if groups > 2 else [], "group", groups, own_a, got_a)
    got_c = scatter_last(begun_c, "group", groups)

    operands = [done_a, own_b] + [x for x, _ in got_b] + [own_c] + [x for x, _ in got_c]
    at_c = 2 + len(got_b)
    out = len(operands)
    pick_b = [(1, None)] + [(2 + i, slot) for i, (_, slot) in enumerate(got_b)]
    pick_c = [(at_c, None)] + [(at_c + 1 + i, slot) for i, (_, slot) in enumerate(got_c)]
    jobs = [
        (out, 0, [(ref, slot, rows_c, ROWS) for ref, slot in pick_c]),
        (out, ROWS, [(0, None, 0, rows_a)]),
        (out, half, [(ref, slot, 0, rows_b) for ref, slot in pick_b]),
        (out, third, [(ref, slot, 0, rows_c) for ref, slot in pick_c]),
    ]
    (gradient,) = add(jobs, operands, [jax.ShapeDtypeStruct((nbox, share), F32)])
    scattered = flush([field_a, field_b, field_c], nbox, got_c[0][0])
    return scattered, gradient


def solution(mesh):
    in_specs = (
        P("tile", "group"),
        P("group", None, "tile", None),
        P("group", None, None),
        P("group", None, "tile", None),
        P(),
        P(),
        P(),
        P(),
    )
    out_specs = (P("group", None, "tile", None), P("tile", "group"))
    return jax.shard_map(
        functools.partial(on_device, mesh.shape["group"], mesh.shape["tile"]),
        mesh=mesh,
        in_specs=in_specs,
        out_specs=out_specs,
        check_vma=False,
    )
```

```python
import functools

import jax
import jax.numpy as jnp
from jax import lax
from jax.experimental import pallas as pl
from jax.experimental.pallas import tpu as pltpu
from jax.sharding import PartitionSpec as P

F32 = jnp.float32
BF16 = jnp.bfloat16
ROWS = 16
VMEM = pl.BlockSpec(memory_space=pltpu.VMEM)
SMEM = pl.BlockSpec(memory_space=pltpu.SMEM)
ANY = pl.BlockSpec(memory_space=pl.ANY)
HBM = pl.BlockSpec(memory_space=pltpu.HBM)


def near(x):
    return pltpu.with_memory_space_constraint(x, pltpu.VMEM)


def far(x):
    return pltpu.with_memory_space_constraint(x, pltpu.HBM)


def split_kernel(runs, whole, *refs):
    outs, sems = refs[:-1], refs[-1]
    copies = [
        pltpu.make_async_copy(
            whole.at[first:first + extent, :], outs[to].at[row:row + extent, :], sems.at[i]
        )
        for i, (to, row, first, extent) in enumerate(runs)
    ]
    for copy in copies:
        copy.start()
    for copy in copies:
        copy.wait()


def split(x, parts):
    runs, shapes = [], []
    for to, part in enumerate(parts):
        row = 0
        for first, extent in part:
            runs.append((to, row, first, extent))
            row += extent
        shapes.append(pltpu.VMEM((row, x.shape[1]), x.dtype))
    return pl.pallas_call(
        functools.partial(split_kernel, runs),
        in_specs=[HBM],
        out_specs=[VMEM] * len(parts),
        out_shape=shapes,
        scratch_shapes=[pltpu.SemaphoreType.DMA((len(runs),))],
        compiler_params=pltpu.CompilerParams(vmem_limit_bytes=4 * 2**20),
        name="split",
    )(far(x))


def encode_kernel(block, group, weighed, signs_in, inc, adj, enc, adjv, part, signs, incv, mix, sems):
    count, nbox, points = incv.shape
    outs = enc.shape[0]
    size = count * group
    steps = nbox // block

    def copies(i):
        rows = pl.ds(pl.multiple_of(i * block, ROWS), block)
        inc_copy = pltpu.make_async_copy(inc.at[0, :, rows, :], incv.at[:, rows, :], sems.at[0, i])
        adj_copy = pltpu.make_async_copy(adj.at[0, :, rows, :], adjv.at[:, rows, :], sems.at[1, i])
        return inc_copy, adj_copy

    signs_copy = pltpu.make_async_copy(signs_in, signs, sems.at[0, steps])
    signs_copy.start()
    for i in range(steps):
        inc_copy, adj_copy = copies(i)
        inc_copy.start()
        if i < weighed:
            adj_copy.start()
    signs_copy.wait()

    r = lax.broadcasted_iota(jnp.int32, (group, size), 0)
    c = lax.broadcasted_iota(jnp.int32, (group, size), 1)
    diagonal = (c % group) == r
    for e in range(outs):
        value = jnp.zeros((group, size), F32)
        for s in range(count):
            value = jnp.where(c // group == s, signs[0, e, s].astype(F32), value)
        mix[e * group:(e + 1) * group, :] = jnp.where(diagonal, value, 0.0).astype(BF16)

    def step(i, carry, weigh):
        inc_copy, adj_copy = copies(i)
        inc_copy.wait()
        if weigh:
            adj_copy.wait()
        for j in range(block // group):
            rows = pl.ds(pl.multiple_of(i * block + j * group, ROWS), group)
            x = incv[:, rows, :].reshape(size, points)
            encoded = jnp.dot(mix[...], x, preferred_element_type=F32).astype(BF16)
            encoded = encoded.reshape(outs, group, points)
            enc[:, rows, :] = encoded
            if weigh:
                part[rows, :] = jnp.sum(adjv[:, rows, :].astype(F32) * encoded.astype(F32), axis=0)
        return carry

    lax.fori_loop(0, weighed, functools.partial(step, weigh=True), 0)
    lax.fori_loop(weighed, steps, functools.partial(step, weigh=False), 0)


def encode(signs, incident, adjoint, weighed, block=32):
    _, count, nbox, points = incident.shape
    outs = adjoint.shape[1]
    group = 256 // count
    return pl.pallas_call(
        functools.partial(encode_kernel, block, group, weighed // block),
        in_specs=[HBM, HBM, HBM],
        out_specs=[VMEM] * 3,
        out_shape=[
            pltpu.VMEM((outs, nbox, points), BF16),
            pltpu.VMEM((outs, nbox, points), BF16),
            pltpu.VMEM((nbox, points), F32),
        ],
        scratch_shapes=[
            pltpu.SMEM(signs.shape, signs.dtype),
            pltpu.VMEM((count, nbox, points), BF16),
            pltpu.VMEM((outs * group, count * group), BF16),
            pltpu.SemaphoreType.DMA((2, nbox // block + 1)),
        ],
        compiler_params=pltpu.CompilerParams(vmem_limit_bytes=12 * 2**20),
        cost_estimate=pl.CostEstimate(
            flops=2 * outs * count * group * nbox * points,
            bytes_accessed=nbox * points * 2 * count,
            transcendentals=0,
        ),
        name="encode",
    )(far(signs), far(incident), far(adjoint))


def weigh_kernel(block, first, adj, enc, _, adj_in, part_in, adjv, part, sems):
    nbox = enc.shape[1]
    steps = nbox // block

    def copy(i):
        rows = pl.ds(pl.multiple_of(i * block, ROWS), block)
        return pltpu.make_async_copy(adj.at[0, :, rows, :], adjv.at[:, rows, :], sems.at[i])

    for i in range(first, steps):
        copy(i).start()

    def step(i, carry):
        copy(i).wait()
        rows = pl.ds(pl.multiple_of(i * block, ROWS), block)
        part[rows, :] = jnp.sum(adjv[:, rows, :].astype(F32) * enc[:, rows, :].astype(F32), axis=0)
        return carry

    lax.fori_loop(first, steps, step, 0)


def weigh(adjoint, enc, adj, part, weighed, after, block=32):
    outs, nbox, points = enc.shape
    return pl.pallas_call(
        functools.partial(weigh_kernel, block, weighed // block),
        in_specs=[HBM] + [VMEM] * 4,
        out_specs=[VMEM, VMEM],
        out_shape=[pltpu.VMEM((outs, nbox, points), BF16), pltpu.VMEM((nbox, points), F32)],
        input_output_aliases={3: 0, 4: 1},
        scratch_shapes=[pltpu.SemaphoreType.DMA((nbox // block,))],
        compiler_params=pltpu.CompilerParams(vmem_limit_bytes=8 * 2**20),
        cost_estimate=pl.CostEstimate(flops=1, bytes_accessed=1, transcendentals=0),
        name="weigh",
    )(far(adjoint), near(enc), near(after), near(adj), near(part))


def add_kernel(jobs, *refs):
    for out, place, terms in jobs:
        value = None
        for ref, slot, first, extent in terms:
            ref = refs[ref]
            x = ref[first:first + extent, :] if slot is None else ref[slot, first:first + extent, :]
            x = x.astype(F32)
            value = x if value is None else value + x
        refs[out][place:place + value.shape[0], :] = value.astype(refs[out].dtype)


def add(jobs, operands, shapes):
    return pl.pallas_call(
        functools.partial(add_kernel, jobs),
        in_specs=[VMEM] * len(operands),
        out_specs=[VMEM] * len(shapes),
        out_shape=shapes,
        compiler_params=pltpu.CompilerParams(vmem_limit_bytes=4 * 2**20),
        name="add",
    )(*map(near, operands))


def leaving(ready, scattered, segments, sems):
    copies, row = [], 0
    for i, (first, size) in enumerate(segments):
        copies.append(
            pltpu.make_async_copy(
                ready.at[:, row:row + size, :], scattered.at[0, :, first:first + size, :], sems.at[i]
            )
        )
        row += size
    return copies


def stage_kernel(axis, count, mine, blocks, edges_at, phases, layout, *refs):
    named, at = {}, 0
    for name, number in layout:
        named[name] = refs[at] if number is None else refs[at:at + number]
        at += 1 if number is None else number
    offsets, mats, expand = named["offsets"], named["mats"], named["expand"]
    adj, part = named["adj"], named["part"]
    padded, ready = named["padded"], named["ready"]
    held, terms = refs[at:]
    outs, nbox, points = adj.shape
    operators, depth, width = mats.shape
    share = points // count
    halves, _, _, lanes = padded.shape
    me = lax.axis_index(axis)
    starts = [pl.multiple_of((me ^ m) * share, share) for m in range(count)]

    def fill(place, extent, values):
        for h in range(halves):
            padded[h, :, place + ROWS:place + ROWS + extent, :] = values[
                :, :, h * lanes:(h + 1) * lanes
            ].astype(F32)

    if mine:
        enc, proj, contrasts = named["enc"], named["proj"], named["pieces"]
        weights = jnp.concatenate([proj[pl.ds(s, share), :] for s in starts], axis=0)
        for runs in mine:
            source = [
                jnp.concatenate(
                    [
                        contrast[row:row + size, :][None]
                        * enc[:, first:first + size, pl.ds(start, share)]
                        for contrast, start in zip(contrasts, starts)
                    ],
                    axis=2,
                )
                for first, row, size in runs
            ]
            total = sum(size for _, _, size in runs)
            source = jnp.concatenate(source, axis=1).reshape(outs * total, points)
            coeffs = jnp.dot(source, weights, preferred_element_type=F32).astype(BF16)
            coeffs = coeffs.reshape(outs, total, width)
            done = 0
            for first, _, size in runs:
                fill(first, size, coeffs[:, done:done + size, :])
                done += size
    for edge, place in zip(named.get("edges", ()), edges_at):
        for h in range(halves):
            edge[:, :, h * lanes:(h + 1) * lanes] = padded[
                h, :, place + ROWS:place + 2 * ROWS, :
            ].astype(BF16)
    if "low" in named:
        fill(-ROWS, ROWS, named["low"][...])
        fill(nbox, ROWS, named["high"][...])

    def translated(first, size):
        moved = [
            padded[h, :, pl.ds(first + ROWS + offsets[t], size), :]
            .astype(BF16)
            .reshape(outs * size, lanes)
            for t in range(operators)
            for h in range(halves)
        ]
        return jnp.dot(
            jnp.concatenate(moved, axis=1),
            mats[...].reshape(operators * depth, width),
            preferred_element_type=F32,
        ).astype(BF16)

    def finish(i, local):
        first, size, row = blocks[i]
        field = jnp.dot(local, expand[...], preferred_element_type=F32)
        field = field.reshape(outs, size, points)
        ready[:, row:row + size, :] = field.astype(BF16)
        terms[0:size, :] = part[first:first + size, :] + jnp.sum(
            adj[:, first:first + size, :].astype(F32) * field, axis=0
        )
        named["own"][row:row + size, :] = terms[0:size, pl.ds(starts[0], share)]
        for phase, members in enumerate(phases):
            for slot, m in enumerate(members):
                named["sent"][phase][slot, row:row + size, :] = terms[
                    0:size, pl.ds(starts[m], share)
                ].astype(BF16)

    rows_of = [outs * size for _, size, _ in blocks]
    held[0, 0:rows_of[0], :] = translated(*blocks[0][:2])
    for i in range(len(blocks)):
        if i + 1 < len(blocks):
            following = translated(*blocks[i + 1][:2])
        finish(i, held[i % 2, 0:rows_of[i], :])
        if i + 1 < len(blocks):
            held[(i + 1) % 2, 0:rows_of[i + 1], :] = following


def stage(axis, count, mine, blocks, edges_at, phases, inputs, state, weight=1.0):
    outs, nbox, points = inputs["adj"].shape
    depth, width = inputs["mats"].shape[1:]
    share = points // count
    lanes = min(128, width)
    placed, rows = [], 0
    for first, size in blocks:
        placed.append((first, size, rows))
        rows += size
    most = max(size for _, size in blocks)

    layout, operands, specs = [], [], []
    for name, value in inputs.items():
        many = isinstance(value, (list, tuple))
        layout.append((name, len(value) if many else None))
        for x in value if many else [value]:
            operands.append(x if name == "offsets" else near(x))
            specs.append(SMEM if name == "offsets" else VMEM)
    aliases = {}
    if state is not None:
        layout.append(("padded_in", None))
        aliases = {len(operands): 0}
        operands.append(near(state))
        specs.append(VMEM)

    layout += [("padded", None), ("ready", None), ("own", None), ("sent", len(phases))]
    out_shape = [
        pltpu.VMEM((width // lanes, outs, nbox + 2 * ROWS, lanes), F32),
        pltpu.VMEM((outs, rows, points), BF16),
        pltpu.VMEM((rows, share), F32),
    ]
    out_shape += [pltpu.VMEM((len(members), rows, share), BF16) for members in phases]
    out_specs = [VMEM] * 3 + [VMEM] * len(phases)
    if edges_at:
        layout.append(("edges", len(edges_at)))
        out_shape += [pltpu.VMEM((outs, ROWS, width), BF16)] * len(edges_at)
        out_specs += [VMEM] * len(edges_at)
    made = sum(size for runs in mine for _, _, size in runs)
    result = pl.pallas_call(
        functools.partial(stage_kernel, axis, count, mine, placed, edges_at, phases, layout),
        in_specs=specs,
        out_specs=out_specs,
        out_shape=out_shape,
        input_output_aliases=aliases,
        scratch_shapes=[
            pltpu.VMEM((2, outs * most, width), BF16),
            pltpu.VMEM((most, points), F32),
        ],
        compiler_params=pltpu.CompilerParams(vmem_limit_bytes=16 * 2**20),
        cost_estimate=pl.CostEstimate(
            flops=int(
                weight * 2 * outs * width
                * (made * points + rows * (inputs["mats"].shape[0] * depth + points))
            ),
            bytes_accessed=int(weight * rows * points * 2 * outs),
            transcendentals=0,
        ),
        name="stage",
    )(*operands)
    padded, ready, own = result[:3]
    return padded, (ready, joined(blocks)), own, result[3:3 + len(phases)], result[3 + len(phases):]


def joined(blocks):
    segments = []
    for first, size in blocks:
        if segments and sum(segments[-1]) == first:
            segments[-1] = (segments[-1][0], segments[-1][1] + size)
        else:
            segments.append((first, size))
    return segments


def flush_kernel(segments, *refs):
    scattered, sems = refs[-2:]
    copies = []
    for ready, held in zip(refs, segments):
        copies += leaving(ready, scattered, held, sems.at[pl.ds(len(copies), len(held))])
    for copy in copies:
        copy.start()
    for copy in copies:
        copy.wait()


def flush(fields, nbox, after):
    outs, _, points = fields[0][0].shape
    segments = [held for _, held in fields]
    return pl.pallas_call(
        functools.partial(flush_kernel, segments),
        in_specs=[VMEM] * (len(fields) + 1),
        out_specs=HBM,
        out_shape=jax.ShapeDtypeStruct((1, outs, nbox, points), BF16),
        scratch_shapes=[pltpu.SemaphoreType.DMA((sum(map(len, segments)),))],
        compiler_params=pltpu.CompilerParams(vmem_limit_bytes=4 * 2**20),
        cost_estimate=pl.CostEstimate(flops=1, bytes_accessed=1, transcendentals=0),
        name="flush",
    )(*[near(ready) for ready, _ in fields], near(after))


def cut_up(first, extent, parts):
    tiles = extent // ROWS
    sizes = [ROWS * (tiles // parts + (i < tiles % parts)) for i in range(parts)]
    return [(first + sum(sizes[:i]), size) for i, size in enumerate(sizes) if size]


def exchange(x, axis, m, count):
    return lax.ppermute(x, axis, [(i, i ^ m) for i in range(count)])


def gather_pieces(pieces, axis, count):
    for m in sorted(range(1, count), key=lambda m: (bin(m).count("1"), -m)):
        if m not in pieces:
            pieces[m] = exchange(pieces[m & (m - 1)], axis, m & -m, count)
    return [pieces[m] for m in range(count)]


def hypercube(count):
    bits = [1 << k for k in range(count.bit_length() - 1)]
    return [[m for m in reversed(range(count)) if m & -m == b] for b in bits]


def folded(members, sent, got, kept):
    for s, m in enumerate(members):
        if m & (m - 1):
            kept[m & (m - 1)] = (kept[m & (m - 1)].astype(F32) + got[s].astype(F32)).astype(BF16)
    return kept


def scatter_steps(sent, axis, count):
    phases = hypercube(count)
    kept = {m: sent[p][s] for p, members in enumerate(phases) for s, m in enumerate(members)}
    final = []
    for p, members in enumerate(phases):
        whole = sent[p] if p == 0 else jnp.stack([kept[m] for m in members])
        got = exchange(whole, axis, 1 << p, count)
        kept = folded(members, sent, got, kept)
        final.append((got, len(members) - 1))
    return final


def first_step(sent, after, axis, count, own=None, got=()):
    phases = hypercube(count)
    came = exchange(sent[0], axis, 1, count)
    rows, share = sent[0].shape[1:]
    operands = [came] + list(sent[1:]) + list(after)
    jobs, shapes, order = [], [], []
    outs = len(operands) + (0 if own is None else 1 + len(got))
    for p, members in enumerate(phases[1:]):
        for s, m in enumerate(members):
            terms = [(1 + p, s, 0, rows)]
            if m + 1 in phases[0]:
                terms.append((0, phases[0].index(m + 1), 0, rows))
            jobs.append((outs + len(order), 0, terms))
            shapes.append(pltpu.VMEM((rows, share), BF16))
            order.append(m)
    if own is not None:
        terms = [(len(operands), None, 0, own.shape[0])]
        terms += [(len(operands) + 1 + i, slot, 0, own.shape[0]) for i, (_, slot) in enumerate(got)]
        jobs.append((outs + len(order), 0, terms))
        shapes.append(pltpu.VMEM(own.shape, F32))
        operands += [own] + [x for x, _ in got]
    result = add(jobs, operands, shapes)
    return (came, dict(zip(order, result))), result[len(order):]


def scatter_last(begun, axis, count):
    came, kept = begun
    phases = hypercube(count)
    final = [(came, len(phases[0]) - 1)]
    for p, members in enumerate(phases):
        if p:
            got = exchange(jnp.stack([kept[m] for m in members]), axis, 1 << p, count)
            kept = folded(members, None, got, kept)
            final.append((got, len(members) - 1))
    return final


def scatter_direct(sent, axis, count):
    return [(exchange(x, axis, m, count), 0) for m, x in enumerate(sent, start=1)]


def on_device(groups, tiles, contrast, incident, signs, adjoint, proj, mats, offsets, expand):
    nbox = contrast.shape[0]
    half = nbox // 32 * 15
    cut, last = half + ROWS, nbox - ROWS
    third = nbox // 32 * 27
    upward = [(i, i + 1) for i in range(tiles - 1)]
    downward = [(i + 1, i) for i in range(tiles - 1)]

    contrast_a, contrast_b = split(contrast, [[(0, cut), (last, ROWS)], [(cut, last - cut)]])
    far_side = groups // 2
    first = exchange(contrast_a, "group", 1, groups)
    top = exchange(contrast_a, "group", far_side, groups)
    weighed = nbox // 8 * 7
    enc, adj, part = encode(signs, incident, adjoint, weighed)
    top, first, enc = lax.optimization_barrier((top, first, enc))
    pieces_a = gather_pieces({0: contrast_a, 1: first, far_side: top}, "group", groups)
    adj, part = weigh(adjoint, enc, adj, part, weighed, top)
    part, contrast_b = lax.optimization_barrier((part, contrast_b))
    pieces_b = [contrast_b] + [exchange(contrast_b, "group", m, groups) for m in range(1, groups)]

    common = dict(offsets=offsets, mats=mats, expand=expand, adj=adj, part=part)
    mine = [[(first, first, size)] for first, size in cut_up(0, cut, 2)]
    mine[-1].append((last, cut, ROWS))
    state, field_a, own_a, sent_a, edges = stage(
        "group", groups, mine, cut_up(ROWS, half - ROWS, 3), (0, last),
        hypercube(groups), common | dict(enc=enc, proj=proj, pieces=pieces_a), None, weight=0.0,
    )
    high = lax.ppermute(edges[0], "tile", downward)
    low = lax.ppermute(edges[1], "tile", upward)

    mine = [[(first, first - cut, size)] for first, size in cut_up(cut, last - cut, 2)]
    state, field_b, own_b, sent_b, _ = stage(
        "group", groups, mine, cut_up(half, third - half, 2), (),
        hypercube(groups), common | dict(enc=enc, proj=proj, pieces=pieces_b), state, weight=1.0,
    )
    got_a = scatter_steps(sent_a, "group", groups)
    _, field_c, own_c, sent_c, _ = stage(
        "group", groups, [], cut_up(third, nbox - third, 2) + [(0, ROWS)], (),
        hypercube(groups), common | dict(low=low, high=high), state, weight=1.0,
    )
    share = own_a.shape[1]
    rows_a, rows_b, rows_c = half - ROWS, third - half, nbox - third
    begun_b, _ = first_step(sent_b, [sent_c[0]], "group", groups)
    got_b = scatter_last(begun_b, "group", groups)
    begun_c, (done_a,) = first_step(sent_c, [begun_b[1][2]] if groups > 2 else [], "group", groups, own_a, got_a)
    got_c = scatter_last(begun_c, "group", groups)

    operands = [done_a, own_b] + [x for x, _ in got_b] + [own_c] + [x for x, _ in got_c]
    at_c = 2 + len(got_b)
    out = len(operands)
    pick_b = [(1, None)] + [(2 + i, slot) for i, (_, slot) in enumerate(got_b)]
    pick_c = [(at_c, None)] + [(at_c + 1 + i, slot) for i, (_, slot) in enumerate(got_c)]
    jobs = [
        (out, 0, [(ref, slot, rows_c, ROWS) for ref, slot in pick_c]),
        (out, ROWS, [(0, None, 0, rows_a)]),
        (out, half, [(ref, slot, 0, rows_b) for ref, slot in pick_b]),
        (out, third, [(ref, slot, 0, rows_c) for ref, slot in pick_c]),
    ]
    (gradient,) = add(jobs, operands, [jax.ShapeDtypeStruct((nbox, share), F32)])
    scattered = flush([field_a, field_b, field_c], nbox, got_c[0][0])
    return scattered, gradient


def solution(mesh):
    in_specs = (
        P("tile", "group"),
        P("group", None, "tile", None),
        P("group", None, None),
        P("group", None, "tile", None),
        P(),
        P(),
        P(),
        P(),
    )
    out_specs = (P("group", None, "tile", None), P("tile", "group"))
    return jax.shard_map(
        functools.partial(on_device, mesh.shape["group"], mesh.shape["tile"]),
        mesh=mesh,
        in_specs=in_specs,
        out_specs=out_specs,
        check_vma=False,
    )
```
